768 devices in a mesh: dp: 24 (over z_hi, x, core), mp: 32 (over y, z_lo).
Axes of the slice: x: 4, y: 8, z: 12 (z_hi: 3, z_lo: 4; z = z_hi * 4 + z_lo), core: 2. Of those that a mesh axis runs over, the one named last changes fastest.
Arguments:
- query_input: bfloat16 [12288, 4096], P('dp', 'mp'), may hold values from -6 to 6
- key_input: bfloat16 [12288, 4096], P('dp', 'mp'), may hold values from -6 to 6
- value_input: bfloat16 [12288, 4096], P('dp', 'mp'), may hold values from -6 to 6
- query_gain: float32 [128], replicated, may hold values from 0.1 to 1.9
- key_gain: float32 [128], replicated, may hold values from 0.1 to 1.9
- out_weight: bfloat16 [4096, 6144], P('mp', 'dp'), may hold values from -0.09375 to 0.09375
- grad_output: bfloat16 [12288, 6144], P(('dp', 'mp')), may hold values from -24 to 24
Outputs:
- grad_query: bfloat16 [12288, 4096], P('dp', 'mp')
- grad_key: bfloat16 [12288, 4096], P('dp', 'mp')
- grad_value: bfloat16 [12288, 4096], P('dp', 'mp')
- grad_weight: bfloat16 [4096, 6144], P('mp', 'dp')
The draws below stay inside these ranges and needn't reach their ends.
All inputs are finite; a program needn't handle non-finite values.
Results may differ from the reference program's by a relative error of at most 0.019.
Values may be sent and summed in bfloat16 or wider, within the bound.
No kernel may reach another device: no remote copies, remote signals or barrier semaphores. Data moves between devices by JAX's collectives and lax.ppermute only.
A program may use at most 32 MiB of HBM per device.

```python
import math
import jax
import jax.numpy as jnp
from jax import lax

D = 6144
DH = 128
PATCH = 256
HEADS = 32
TOK_DEV = 512
TOKENS = 12288
N_DP = 24


def with_spikes(entries, stream_key, source, target, blocks, factor):
    owner, partner = [(jnp.arange(entries.shape[position]) // (entries.shape[position] // blocks)).reshape([-1 if axis == position else 1 for axis in range(entries.ndim)]) for position in (source, target)]
    chosen = jax.random.permutation(stream_key, blocks)[partner]
    strong = (owner == chosen) | (owner == (partner + blocks // 2) % blocks)
    return jnp.where(strong, factor * entries, entries)


def block_scale(stream_key, dims, shards, low, largest):
    loudness = 1.0
    for axis_at, shards_of in shards:
        heights = jax.random.uniform(jax.random.fold_in(jax.random.fold_in(stream_key, 6), axis_at), (shards_of,), jnp.float32, low / len(shards), largest / len(shards))
        loudness = loudness * jnp.repeat(jnp.exp(heights), dims[axis_at] // shards_of).reshape((-1,) + (1,) * (len(dims) - 1 - axis_at))
    return loudness


def noise(rng, dims, deviation, most, cuts=(), held_as=jnp.bfloat16):
    drawn = deviation * jax.random.normal(rng, dims, jnp.float32)
    if cuts:
        drawn = drawn * block_scale(rng, dims, cuts, -0.22, 0.18)
    return jnp.clip(drawn, -most, most).astype(held_as)


def gaussian_with(own_key, dims, scale, most, split, heavy, kind=jnp.bfloat16):
    drawn = scale * jax.random.normal(own_key, dims, jnp.float32)
    if split:
        drawn = drawn * block_scale(own_key, dims, split, -0.22, 0.18)
    return jnp.clip(with_spikes(drawn, jax.random.fold_in(own_key, 3), *heavy), -most, most).astype(kind)


def setup_inputs(seed: int = 0) -> dict:
    key_list = jax.random.split(jax.random.key(seed), 8)
    query_input = noise(key_list[0], (TOKENS, HEADS * DH), 1.0, 6.0, ((0, 24), (1, 32)))
    key_input = noise(key_list[1], (TOKENS, HEADS * DH), 1.0, 6.0, ((0, 24), (1, 32)))
    value_input = noise(key_list[2], (TOKENS, HEADS * DH), 1.0, 6.0, ((0, 24), (1, 32)))
    query_gain = jnp.clip(1.0 + 0.18 * jax.random.normal(key_list[3], (DH,), jnp.float32), 0.1, 1.9)
    key_gain = jnp.clip(1.0 + 0.18 * jax.random.normal(key_list[4], (DH,), jnp.float32), 0.1, 1.9)
    out_weight = noise(key_list[5], (HEADS * DH, D), (HEADS * DH) ** -0.5, 0.09375, ((0, 32), (1, 24)))
    grad_output = gaussian_with(key_list[6], (TOKENS, D), 1.0, 24.0, ((0, 768),), (0, 1, 768, 6.0))
    return {"query_input": query_input, "key_input": key_input, "value_input": value_input, "query_gain": query_gain, "key_gain": key_gain, "out_weight": out_weight, "grad_output": grad_output}


epsilon = 1e-06

def normalize(inputs, gain):
    inputs = inputs.astype(jnp.float32)
    average = lax.optimization_barrier(jnp.mean(inputs, axis=-1, keepdims=True))
    centred = inputs - average
    inverse = lax.rsqrt(lax.optimization_barrier(jnp.mean(centred * centred, axis=-1, keepdims=True)) + epsilon)
    unit_rows = centred * inverse
    return (unit_rows, inverse, unit_rows * gain)

def norm_back(gradient, unit_rows, inverse, gain):
    scaled = gradient * gain
    return (scaled - lax.optimization_barrier(jnp.mean(scaled, axis=-1, keepdims=True)) - unit_rows * lax.optimization_barrier(jnp.mean(scaled * unit_rows, axis=-1, keepdims=True))) * inverse

def attend(query_input, key_input, value_input, grad_heads, query_gain, key_gain):
    scaling = 1.0 / math.sqrt(query_input.shape[-1])
    query_unit, query_inv, query_normed = normalize(query_input, query_gain)
    key_unit, key_inv, key_normed = normalize(key_input, key_gain)
    query_low = query_normed.astype(jnp.bfloat16).astype(jnp.float32)
    key_low = key_normed.astype(jnp.bfloat16).astype(jnp.float32)
    scores = jnp.einsum('iphd,ikhd->ihpk', query_low, key_low) * scaling
    exponent = jnp.exp(scores)
    attention = exponent / lax.optimization_barrier(jnp.sum(exponent, axis=-1, keepdims=True))
    attention_low = attention.astype(jnp.bfloat16).astype(jnp.float32)
    value_wide = value_input.astype(jnp.float32)
    heads_wide = grad_heads.astype(jnp.float32)
    mixed = jnp.einsum('ihpk,ikhd->iphd', attention_low, value_wide).astype(jnp.bfloat16)
    grad_value = jnp.einsum('ihpk,iphd->ikhd', attention_low, heads_wide).astype(jnp.bfloat16)
    grad_attention = jnp.einsum('iphd,ikhd->ihpk', heads_wide, value_wide)
    row_delta = lax.optimization_barrier(jnp.sum(attention * grad_attention, axis=-1, keepdims=True))
    grad_scores = (attention * (grad_attention - row_delta)).astype(jnp.bfloat16).astype(jnp.float32)
    grad_qn = jnp.einsum('ihpk,ikhd->iphd', grad_scores, key_low) * scaling
    grad_kn = jnp.einsum('ihpk,iphd->ikhd', grad_scores, query_low) * scaling
    grad_query = norm_back(grad_qn, query_unit, query_inv, query_gain).astype(jnp.bfloat16)
    grad_key = norm_back(grad_kn, key_unit, key_inv, key_gain).astype(jnp.bfloat16)
    return (mixed, grad_query, grad_key, grad_value)

def reference(query_input, key_input, value_input, query_gain, key_gain, out_weight, grad_output):
    grad_heads = jnp.dot(grad_output, out_weight.T, preferred_element_type=jnp.float32).astype(jnp.bfloat16)
    head_shape = (TOKENS // PATCH, PATCH, HEADS, DH)

    def per_image(inputs_one):
        results = attend(*(entry[None] for entry in inputs_one), query_gain, key_gain)
        return tuple((entry[0] for entry in results))
    stacked = tuple((entry.reshape(head_shape) for entry in (query_input, key_input, value_input, grad_heads)))
    mixed, grad_query, grad_key, grad_value = lax.map(per_image, stacked)
    mixed = mixed.reshape(TOKENS, HEADS * DH)
    mixed_groups = mixed.reshape(N_DP, TOK_DEV, HEADS * DH)
    grad_groups = grad_output.reshape(N_DP, TOK_DEV, D)

    def accumulate(summed, inputs_one):
        product = jnp.dot(inputs_one[0].T, inputs_one[1], preferred_element_type=jnp.float32).astype(jnp.bfloat16)
        product = lax.optimization_barrier(product)
        return (summed + product.astype(jnp.float32), None)
    summed, _ = lax.scan(accumulate, jnp.zeros((HEADS * DH, D), jnp.float32), (mixed_groups, grad_groups))
    flat = (TOKENS, HEADS * DH)
    return (grad_query.reshape(flat), grad_key.reshape(flat), grad_value.reshape(flat), summed.astype(jnp.bfloat16))
```

```python
import functools
import math

import jax
import jax.numpy as jnp
from jax import lax
from jax.experimental import pallas as pl
from jax.experimental.pallas import tpu as pltpu
from jax.sharding import Mesh
from jax.sharding import PartitionSpec as P

DH = 128
PATCH = 256
IMAGES = 2
TOK = 512
NZ, NX, NC, NY, NL = 3, 4, 2, 8, 4
BLK = 256
WIDE = NZ * NC * BLK
epsilon = 1e-06
F32 = jnp.float32
BF16 = jnp.bfloat16
VMEM_LIMIT = 32 * 1024 * 1024
SCALING = 1.0 / math.sqrt(DH)


def dot(a, b, ca, cb):
    return lax.dot_general(a, b, (((ca,), (cb,)), ((), ())), preferred_element_type=F32)


def normalize(inputs):
    inputs = inputs.astype(F32)
    average = jnp.mean(inputs, axis=-1, keepdims=True)
    centred = inputs - average
    inverse = lax.rsqrt(jnp.mean(centred * centred, axis=-1, keepdims=True) + epsilon)
    return centred * inverse, inverse


def norm_back(gradient, unit_rows, inverse, gain):
    scaled = gradient * gain
    return (
        scaled
        - jnp.mean(scaled, axis=-1, keepdims=True)
        - unit_rows * jnp.mean(scaled * unit_rows, axis=-1, keepdims=True)
    ) * inverse


def forward_kernel(q_ref, k_ref, v_ref, qg_ref, kg_ref, mixed_ref, att_ref):
    for image in range(IMAGES):
        rows = pl.ds(image * PATCH, PATCH)
        query_low = (normalize(q_ref[rows, :])[0] * qg_ref[...]).astype(BF16)
        key_low = (normalize(k_ref[rows, :])[0] * kg_ref[...]).astype(BF16)
        exponent = jnp.exp(dot(query_low, key_low, 1, 1) * SCALING)
        attention = exponent / jnp.sum(exponent, axis=-1, keepdims=True)
        att_ref[image] = attention
        mixed = dot(v_ref[rows, :], attention.astype(BF16), 0, 1)
        mixed_ref[:, rows] = mixed.astype(BF16)


def backward_kernel(
    q_ref, k_ref, v_ref, qg_ref, kg_ref, att_ref, gh_ref, dq_ref, dk_ref, dv_ref
):
    for image in range(IMAGES):
        rows = pl.ds(image * PATCH, PATCH)
        total = gh_ref[0, rows, :].astype(F32)
        for part in range(1, NL):
            total = total + gh_ref[part, rows, :].astype(F32)
        grad_heads = total.astype(BF16)
        query_unit, query_inv = normalize(q_ref[rows, :])
        key_unit, key_inv = normalize(k_ref[rows, :])
        query_low = (query_unit * qg_ref[...]).astype(BF16)
        key_low = (key_unit * kg_ref[...]).astype(BF16)
        attention = att_ref[image]
        dv_ref[rows, :] = dot(attention.astype(BF16), grad_heads, 0, 0).astype(BF16)
        grad_attention = dot(grad_heads, v_ref[rows, :], 1, 1)
        row_delta = jnp.sum(attention * grad_attention, axis=-1, keepdims=True)
        grad_scores = (attention * (grad_attention - row_delta)).astype(BF16)
        grad_qn = dot(grad_scores, key_low, 1, 0) * SCALING
        grad_kn = dot(grad_scores, query_low, 0, 0) * SCALING
        dq_ref[rows, :] = norm_back(grad_qn, query_unit, query_inv, qg_ref[...]).astype(BF16)
        dk_ref[rows, :] = norm_back(grad_kn, key_unit, key_inv, kg_ref[...]).astype(BF16)


def block(ref, zone, core):
    start = pl.multiple_of(lax.rem(zone, NZ) * (NC * BLK) + core * BLK, BLK)
    return ref[:, pl.ds(start, BLK)]


def heads_kernel(g_ref, own_ref, other_ref, out_ref):
    zone, core = lax.axis_index("zh"), lax.axis_index("core")
    total = None
    for ref, side in ((own_ref, core), (other_ref, 1 - core)):
        for step in range(NZ):
            weight = ref[:, step].reshape(NX * DH, BLK)
            term = dot(block(g_ref, zone + NZ - step, side), weight, 1, 1)
            total = term if total is None else total + term
    for head in range(NL):
        out_ref[head] = total[:, head * DH : (head + 1) * DH].astype(BF16)


def weight_kernel(g_ref, mixed_ref, keep_ref, send_ref):
    zone, core = lax.axis_index("zh"), lax.axis_index("core")
    mixed = mixed_ref[...]
    for ref, side in ((send_ref, 1 - core), (keep_ref, core)):
        for step in range(NZ):
            term = dot(mixed, block(g_ref, zone + step, side), 1, 0)
            ref[:, step] = term.reshape(NL, DH, BLK).astype(ref.dtype)


def call(kernel, outs, flops, moved, *operands):
    return pl.pallas_call(
        kernel,
        out_shape=outs,
        in_specs=[pl.BlockSpec(memory_space=pltpu.VMEM)] * len(operands),
        out_specs=jax.tree.map(lambda _: pl.BlockSpec(memory_space=pltpu.VMEM), outs),
        compiler_params=pltpu.CompilerParams(vmem_limit_bytes=VMEM_LIMIT),
        cost_estimate=pl.CostEstimate(flops=flops, bytes_accessed=moved, transcendentals=0),
    )(*operands)


def crossing(shift):
    pairs = []
    for zone in range(NZ):
        for across in range(NX):
            for low in range(NL):
                target = (zone + shift) % NZ
                pairs.append(
                    ((zone * NX + across) * NL + low, (target * NX + low) * NL + across)
                )
    return pairs


def cross(entry, shift):
    return lax.ppermute(entry, ("zh", "x", "zl"), crossing(shift))


def swap_cores(entry):
    return lax.ppermute(entry, "core", [(0, 1), (1, 0)])


def shards(query_input, key_input, value_input, query_gain, key_gain, out_weight, grad_output):
    query_gain = query_gain.reshape(1, DH)
    key_gain = key_gain.reshape(1, DH)
    shape = jax.ShapeDtypeStruct

    rows = grad_output.shape[0]
    pieces = grad_output.reshape(rows, NZ, NL, NC * BLK).transpose(2, 0, 1, 3)
    pieces = pieces.reshape(NL * rows, WIDE)
    exchanged = lax.all_to_all(pieces, "zl", 0, 0, tiled=True)
    gathered = lax.all_gather(exchanged, "y", axis=0, tiled=True)

    moved = jnp.stack([cross(out_weight, shift) for shift in range(NZ)])
    own = lax.all_gather(moved, "x", axis=0)
    other = swap_cores(own)

    mixed, attention = call(
        forward_kernel,
        (shape((DH, TOK), BF16), shape((IMAGES, PATCH, PATCH), F32)),
        2 * 2 * IMAGES * PATCH * PATCH * DH,
        1 << 20,
        query_input,
        key_input,
        value_input,
        query_gain,
        key_gain,
    )
    mixed_all = lax.all_gather(mixed, "zl", axis=0, tiled=True)

    gathered, mixed_all, own, other = lax.optimization_barrier(
        (gathered, mixed_all, own, other)
    )
    keep, send = call(
        weight_kernel,
        (shape((NL, NZ, DH, BLK), F32), shape((NL, NZ, DH, BLK), BF16)),
        2 * TOK * TOK * WIDE,
        5 << 20,
        gathered,
        mixed_all,
    )
    received = swap_cores(send)
    partial = call(
        heads_kernel,
        shape((NL, TOK, DH), BF16),
        2 * TOK * TOK * WIDE,
        4 << 20,
        gathered,
        own,
        other,
    )
    grad_heads = lax.all_to_all(partial, "zl", 0, 0, tiled=True)

    summed = (keep + received.astype(F32)).astype(BF16)
    spread = lax.all_to_all(summed, "x", 0, 0, tiled=True)
    by_zone = sum(spread[part].astype(F32) for part in range(NX)).astype(BF16)
    last = [cross(by_zone[shift], shift) for shift in range(NZ)]
    grad_weight = sum(entry.astype(F32) for entry in last).astype(BF16)

    grad_query, grad_key, grad_value = call(
        backward_kernel,
        (shape((TOK, DH), BF16),) * 3,
        5 * 2 * IMAGES * PATCH * PATCH * DH,
        2 << 20,
        query_input,
        key_input,
        value_input,
        query_gain,
        key_gain,
        attention,
        grad_heads,
    )
    return grad_query, grad_key, grad_value, grad_weight


def solution(mesh):
    axes = ("zh", "x", "core", "y", "zl")
    fine = Mesh(mesh.devices.reshape(NZ, NX, NC, NY, NL), axes)
    tokens, heads = ("zh", "x", "core"), ("y", "zl")
    in_specs = (
        P(tokens, heads),
        P(tokens, heads),
        P(tokens, heads),
        P(),
        P(),
        P(heads, tokens),
        P(tokens + heads, None),
    )
    out_specs = (P(tokens, heads), P(tokens, heads), P(tokens, heads), P(heads, tokens))
    return jax.shard_map(shards, mesh=fine, in_specs=in_specs, out_specs=out_specs, check_vma=False)
```

```python
import functools
import math

import jax
import jax.numpy as jnp
from jax import lax
from jax.experimental import pallas as pl
from jax.experimental.pallas import tpu as pltpu
from jax.sharding import Mesh
from jax.sharding import PartitionSpec as P

DH = 128
PATCH = 256
IMAGES = 2
TOK = 512
NZ, NX, NC, NY, NL = 3, 4, 2, 8, 4
BLK = 256
WIDE = NZ * BLK
epsilon = 1e-06
F32 = jnp.float32
BF16 = jnp.bfloat16
VMEM_LIMIT = 32 * 1024 * 1024
SCALING = 1.0 / math.sqrt(DH)


def dot(a, b, ca, cb):
    return lax.dot_general(a, b, (((ca,), (cb,)), ((), ())), preferred_element_type=F32)


def normalize(inputs):
    inputs = inputs.astype(F32)
    average = jnp.mean(inputs, axis=-1, keepdims=True)
    centred = inputs - average
    inverse = lax.rsqrt(jnp.mean(centred * centred, axis=-1, keepdims=True) + epsilon)
    return centred * inverse, inverse


def norm_back(gradient, unit_rows, inverse, gain):
    scaled = gradient * gain
    return (
        scaled
        - jnp.mean(scaled, axis=-1, keepdims=True)
        - unit_rows * jnp.mean(scaled * unit_rows, axis=-1, keepdims=True)
    ) * inverse


def forward_kernel(q_ref, k_ref, v_ref, qg_ref, kg_ref, mixed_ref, att_ref):
    for image in range(IMAGES):
        rows = pl.ds(image * PATCH, PATCH)
        query_low = (normalize(q_ref[rows, :])[0] * qg_ref[...]).astype(BF16)
        key_low = (normalize(k_ref[rows, :])[0] * kg_ref[...]).astype(BF16)
        exponent = jnp.exp(dot(query_low, key_low, 1, 1) * SCALING)
        attention = exponent / jnp.sum(exponent, axis=-1, keepdims=True)
        att_ref[image] = attention
        mixed = dot(v_ref[rows, :], attention.astype(BF16), 0, 1)
        mixed_ref[:, rows] = mixed.astype(BF16)


def backward_kernel(
    q_ref, k_ref, v_ref, qg_ref, kg_ref, att_ref, gh_ref, dq_ref, dk_ref, dv_ref
):
    for image in range(IMAGES):
        rows = pl.ds(image * PATCH, PATCH)
        total = gh_ref[0, rows, :].astype(F32)
        for part in range(1, NY):
            total = total + gh_ref[part, rows, :].astype(F32)
        grad_heads = total.astype(BF16)
        query_unit, query_inv = normalize(q_ref[rows, :])
        key_unit, key_inv = normalize(k_ref[rows, :])
        query_low = (query_unit * qg_ref[...]).astype(BF16)
        key_low = (key_unit * kg_ref[...]).astype(BF16)
        attention = att_ref[image]
        dv_ref[rows, :] = dot(attention.astype(BF16), grad_heads, 0, 0).astype(BF16)
        grad_attention = dot(grad_heads, v_ref[rows, :], 1, 1)
        row_delta = jnp.sum(attention * grad_attention, axis=-1, keepdims=True)
        grad_scores = (attention * (grad_attention - row_delta)).astype(BF16)
        grad_qn = dot(grad_scores, key_low, 1, 0) * SCALING
        grad_kn = dot(grad_scores, query_low, 0, 0) * SCALING
        dq_ref[rows, :] = norm_back(grad_qn, query_unit, query_inv, qg_ref[...]).astype(BF16)
        dk_ref[rows, :] = norm_back(grad_kn, key_unit, key_inv, kg_ref[...]).astype(BF16)


def assemble(g_refs, held_ref):
    low = lax.axis_index("zl")
    for step in range(NL):
        held_ref[low ^ step] = g_refs[step][...]


def block(ref, zone):
    columns = pl.ds(zone * BLK, BLK)
    parts = [ref[:, line, :, columns].reshape(-1, BLK) for line in range(NY)]
    return jnp.concatenate(parts, axis=0)


def heads_kernel(*refs):
    g_refs, own_refs, other_refs = refs[:NL], refs[NL : NL + NX], refs[NL + NX : NL + 2 * NX]
    out_ref, held_ref = refs[-2:]
    assemble(g_refs, held_ref)
    here, core, across = (lax.axis_index(name) for name in ("zh", "core", "x"))
    blocks = [block(held_ref, lax.rem(here + NZ - zone, NZ)) for zone in range(NZ)]
    for step in range(NX):
        for part_refs, side in ((own_refs, core), (other_refs, 1 - core)):
            total = None
            for zone in range(NZ):
                term = dot(blocks[zone], part_refs[step][zone], 1, 1)
                total = term if total is None else total + term
            head = NC * lax.rem(across + NX - step, NX) + side
            out_ref[head] = total.astype(BF16)


def weight_kernel(*refs):
    g_refs, mixed_ref = refs[:NL], refs[NL]
    keep_ref, send_ref, held_ref = refs[-3:]
    assemble(g_refs, held_ref)
    here, core, across = (lax.axis_index(name) for name in ("zh", "core", "x"))
    blocks = [block(held_ref, lax.rem(here + step, NZ)) for step in range(NZ)]
    for ref, side in ((send_ref, 1 - core), (keep_ref, core)):
        parts = [mixed_ref[lax.rem(across + step, NX), side] for step in range(NX)]
        mixed = jnp.concatenate(parts, axis=0)
        for step in range(NZ):
            term = dot(mixed, blocks[step], 1, 0)
            ref[:, step] = term.reshape(NX, DH, BLK).astype(ref.dtype)


def call(kernel, outs, flops, moved, operands, scratch=()):
    return pl.pallas_call(
        kernel,
        out_shape=outs,
        in_specs=[pl.BlockSpec(memory_space=pltpu.VMEM)] * len(operands),
        out_specs=jax.tree.map(lambda _: pl.BlockSpec(memory_space=pltpu.VMEM), outs),
        scratch_shapes=list(scratch),
        compiler_params=pltpu.CompilerParams(vmem_limit_bytes=VMEM_LIMIT),
        cost_estimate=pl.CostEstimate(flops=flops, bytes_accessed=moved, transcendentals=0),
    )(*operands)


def cross(entry, shift):
    pairs = []
    for zone in range(NZ):
        for across in range(NX * NC):
            for line in range(NY):
                target = (zone + shift) % NZ
                pairs.append(
                    ((zone * NX * NC + across) * NY + line, (target * NX * NC + line) * NY + across)
                )
    return lax.ppermute(entry, ("zh", "x", "core", "y"), pairs)


def shifted(entry, axis, size, step):
    return lax.ppermute(entry, axis, [(at, (at + step) % size) for at in range(size)])


def flipped(entry, axis, size, step):
    return lax.ppermute(entry, axis, [(at, at ^ step) for at in range(size)])


def swap_cores(entry):
    return lax.ppermute(entry, "core", [(0, 1), (1, 0)])


def shards(query_input, key_input, value_input, query_gain, key_gain, out_weight, grad_output):
    query_gain = query_gain.reshape(1, DH)
    key_gain = key_gain.reshape(1, DH)
    shape = jax.ShapeDtypeStruct

    mixed, attention = call(
        forward_kernel,
        (shape((DH, TOK), BF16), shape((IMAGES, PATCH, PATCH), F32)),
        2 * 2 * IMAGES * PATCH * PATCH * DH,
        1 << 20,
        (query_input, key_input, value_input, query_gain, key_gain),
    )
    rows = grad_output.shape[0]
    pieces = grad_output.reshape(rows, NZ, NY, BLK).transpose(2, 0, 1, 3)
    pieces = pieces.reshape(NY, rows, WIDE)
    pieces, mixed = lax.optimization_barrier((pieces, mixed))
    mixed_all = lax.all_gather(mixed, "y", axis=0, tiled=True)
    exchanged = lax.all_to_all(pieces, "y", 0, 0, tiled=True)
    crossed = cross(out_weight, 0)
    exchanged, crossed = lax.optimization_barrier((exchanged, crossed))
    zones = [crossed] + [shifted(crossed, "zh", NZ, step) for step in range(1, NZ)]
    gathered = [exchanged] + [flipped(exchanged, "zl", NL, step) for step in range(1, NL)]
    zones = jnp.stack(zones)
    own = [zones] + [shifted(zones, "x", NX, step) for step in range(1, NX)]
    gathered, mixed_all, own = lax.optimization_barrier((gathered, mixed_all, own))
    other = [swap_cores(entry) for entry in own]

    half = (NX, NZ, DH, BLK)
    held = (pltpu.VMEM((NL, NY, rows, WIDE), BF16),)
    keep, send = call(
        weight_kernel,
        (shape(half, F32), shape(half, BF16)),
        2 * TOK * NY * DH * WIDE,
        5 << 20,
        (*gathered, mixed_all.reshape(NX, NC, DH, TOK)),
        held,
    )
    received = swap_cores(send)
    partial = call(
        heads_kernel,
        shape((NY, TOK, DH), BF16),
        2 * TOK * NY * DH * WIDE,
        4 << 20,
        (*gathered, *own, *other),
        held,
    )
    grad_heads = lax.all_to_all(partial, "y", 0, 0, tiled=True)

    summed = [(keep[step] + received[step].astype(F32)).astype(BF16) for step in range(NX)]
    spread = [summed[0]] + [shifted(summed[step], "x", NX, step) for step in range(1, NX)]
    by_zone = sum(entry.astype(F32) for entry in spread).astype(BF16)
    last = [cross(by_zone[shift], shift) for shift in range(NZ)]
    grad_weight = sum(entry.astype(F32) for entry in last).astype(BF16)

    grad_query, grad_key, grad_value = call(
        backward_kernel,
        (shape((TOK, DH), BF16),) * 3,
        5 * 2 * IMAGES * PATCH * PATCH * DH,
        2 << 20,
        (query_input, key_input, value_input, query_gain, key_gain, attention, grad_heads),
    )
    return grad_query, grad_key, grad_value, grad_weight


def solution(mesh):
    axes = ("zh", "x", "core", "y", "zl")
    fine = Mesh(mesh.devices.reshape(NZ, NX, NC, NY, NL), axes)
    tokens, heads = ("zh", "x", "core"), ("y", "zl")
    in_specs = (
        P(tokens, heads),
        P(tokens, heads),
        P(tokens, heads),
        P(),
        P(),
        P(heads, tokens),
        P(tokens + heads, None),
    )
    out_specs = (P(tokens, heads), P(tokens, heads), P(tokens, heads), P(heads, tokens))
    return jax.shard_map(shards, mesh=fine, in_specs=in_specs, out_specs=out_specs, check_vma=False)
```

```python
import functools
import math

import jax
import jax.numpy as jnp
from jax import lax
from jax.experimental import pallas as pl
from jax.experimental.pallas import tpu as pltpu
from jax.sharding import Mesh
from jax.sharding import PartitionSpec as P

DH = 128
PATCH = 256
IMAGES = 2
TOK = 512
NZ, NX, NC, NY, NL = 3, 4, 2, 8, 4
BLK = 256
WIDE = NZ * BLK
epsilon = 1e-06
F32 = jnp.float32
BF16 = jnp.bfloat16
VMEM_LIMIT = 32 * 1024 * 1024
SCALING = 1.0 / math.sqrt(DH)


def dot(a, b, ca, cb):
    return lax.dot_general(a, b, (((ca,), (cb,)), ((), ())), preferred_element_type=F32)


def normalize(inputs):
    inputs = inputs.astype(F32)
    average = jnp.mean(inputs, axis=-1, keepdims=True)
    centred = inputs - average
    inverse = lax.rsqrt(jnp.mean(centred * centred, axis=-1, keepdims=True) + epsilon)
    return centred * inverse, inverse


def norm_back(gradient, unit_rows, inverse, gain):
    scaled = gradient * gain
    return (
        scaled
        - jnp.mean(scaled, axis=-1, keepdims=True)
        - unit_rows * jnp.mean(scaled * unit_rows, axis=-1, keepdims=True)
    ) * inverse


def forward_kernel(q_ref, k_ref, v_ref, qg_ref, kg_ref, go_ref, mixed_ref, att_ref, cut_ref):
    for zone in range(NZ):
        for line in range(NY):
            source = (zone * NY + line) * BLK
            cut_ref[line, :, zone * BLK : (zone + 1) * BLK] = go_ref[:, source : source + BLK]
    for image in range(IMAGES):
        rows = pl.ds(image * PATCH, PATCH)
        query_low = (normalize(q_ref[rows, :])[0] * qg_ref[...]).astype(BF16)
        key_low = (normalize(k_ref[rows, :])[0] * kg_ref[...]).astype(BF16)
        exponent = jnp.exp(dot(query_low, key_low, 1, 1) * SCALING)
        attention = exponent / jnp.sum(exponent, axis=-1, keepdims=True)
        att_ref[image] = attention
        mixed = dot(v_ref[rows, :], attention.astype(BF16), 0, 1)
        mixed_ref[:, rows] = mixed.astype(BF16)


def backward_kernel(
    q_ref, k_ref, v_ref, qg_ref, kg_ref, att_ref, gh_ref, dq_ref, dk_ref, dv_ref
):
    for image in range(IMAGES):
        rows = pl.ds(image * PATCH, PATCH)
        total = gh_ref[0, rows, :].astype(F32)
        for part in range(1, NY):
            total = total + gh_ref[part, rows, :].astype(F32)
        grad_heads = total.astype(BF16)
        query_unit, query_inv = normalize(q_ref[rows, :])
        key_unit, key_inv = normalize(k_ref[rows, :])
        query_low = (query_unit * qg_ref[...]).astype(BF16)
        key_low = (key_unit * kg_ref[...]).astype(BF16)
        attention = att_ref[image]
        dv_ref[rows, :] = dot(attention.astype(BF16), grad_heads, 0, 0).astype(BF16)
        grad_attention = dot(grad_heads, v_ref[rows, :], 1, 1)
        row_delta = jnp.sum(attention * grad_attention, axis=-1, keepdims=True)
        grad_scores = (attention * (grad_attention - row_delta)).astype(BF16)
        grad_qn = dot(grad_scores, key_low, 1, 0) * SCALING
        grad_kn = dot(grad_scores, query_low, 0, 0) * SCALING
        dq_ref[rows, :] = norm_back(grad_qn, query_unit, query_inv, qg_ref[...]).astype(BF16)
        dk_ref[rows, :] = norm_back(grad_kn, key_unit, key_inv, kg_ref[...]).astype(BF16)


def block(ref, zone):
    columns = pl.ds(zone * BLK, BLK)
    parts = [ref[:, line, :, columns].reshape(-1, BLK) for line in range(NY)]
    return jnp.concatenate(parts, axis=0)


def heads_kernel(g_ref, own_ref, other_ref, out_ref):
    here, core = lax.axis_index("zh"), lax.axis_index("core")
    blocks = [block(g_ref, lax.rem(here + NZ - step, NZ)) for step in range(NZ)]
    for ref, side in ((own_ref, core), (other_ref, 1 - core)):
        total = None
        for step in range(NZ):
            term = dot(blocks[step], ref[:, step].reshape(NX * DH, BLK), 1, 1)
            total = term if total is None else total + term
        for across in range(NX):
            piece = total[:, across * DH : (across + 1) * DH]
            out_ref[NC * across + side] = piece.astype(BF16)


def weight_kernel(g_ref, mixed_ref, keep_ref, send_ref):
    here, core, across = (lax.axis_index(name) for name in ("zh", "core", "x"))
    blocks = [block(g_ref, lax.rem(here + step, NZ)) for step in range(NZ)]
    for ref, side in ((send_ref, 1 - core), (keep_ref, core)):
        parts = [mixed_ref[lax.rem(across + step, NX), side] for step in range(NX)]
        mixed = jnp.concatenate(parts, axis=0)
        for step in range(NZ):
            term = dot(mixed, blocks[step], 1, 0)
            ref[:, step] = term.reshape(NX, DH, BLK).astype(ref.dtype)


def call(kernel, outs, flops, moved, operands):
    return pl.pallas_call(
        kernel,
        out_shape=outs,
        in_specs=[pl.BlockSpec(memory_space=pltpu.VMEM)] * len(operands),
        out_specs=jax.tree.map(lambda _: pl.BlockSpec(memory_space=pltpu.VMEM), outs),
        compiler_params=pltpu.CompilerParams(vmem_limit_bytes=VMEM_LIMIT),
        cost_estimate=pl.CostEstimate(flops=flops, bytes_accessed=moved, transcendentals=0),
    )(*operands)


def cross(entry, shift):
    pairs = []
    for zone in range(NZ):
        for across in range(NX * NC):
            for line in range(NY):
                target = (zone + shift) % NZ
                pairs.append(
                    ((zone * NX * NC + across) * NY + line, (target * NX * NC + line) * NY + across)
                )
    return lax.ppermute(entry, ("zh", "x", "core", "y"), pairs)


def shifted(entry, axis, size, step):
    return lax.ppermute(entry, axis, [(at, (at + step) % size) for at in range(size)])


def swap_cores(entry):
    return lax.ppermute(entry, "core", [(0, 1), (1, 0)])


def shards(query_input, key_input, value_input, query_gain, key_gain, out_weight, grad_output):
    query_gain = query_gain.reshape(1, DH)
    key_gain = key_gain.reshape(1, DH)
    shape = jax.ShapeDtypeStruct

    rows = grad_output.shape[0]
    mixed, attention, pieces = call(
        forward_kernel,
        (
            shape((DH, TOK), BF16),
            shape((IMAGES, PATCH, PATCH), F32),
            shape((NY, rows, WIDE), BF16),
        ),
        2 * 2 * IMAGES * PATCH * PATCH * DH,
        1 << 20,
        (query_input, key_input, value_input, query_gain, key_gain, grad_output),
    )
    mixed_all = lax.all_gather(mixed, "y", axis=0, tiled=True)
    exchanged = lax.all_to_all(pieces, "y", 0, 0, tiled=True)
    crossed = jnp.stack([cross(out_weight, shift) for shift in range(NZ)])
    exchanged, crossed = lax.optimization_barrier((exchanged, crossed))
    copies = jnp.broadcast_to(crossed[None], (NX,) + crossed.shape)
    own = lax.all_to_all(copies, "x", 0, 0, tiled=True)
    gathered = lax.all_gather(exchanged, "zl", axis=0)
    gathered, mixed_all, own = lax.optimization_barrier((gathered, mixed_all, own))
    other = swap_cores(own)

    half = (NX, NZ, DH, BLK)
    keep, send = call(
        weight_kernel,
        (shape(half, F32), shape(half, BF16)),
        2 * TOK * NY * DH * WIDE,
        5 << 20,
        (gathered, mixed_all.reshape(NX, NC, DH, TOK)),
    )
    received = swap_cores(send)
    partial = call(
        heads_kernel,
        shape((NY, TOK, DH), BF16),
        2 * TOK * NY * DH * WIDE,
        4 << 20,
        (gathered, own, other),
    )
    summed = [(keep[step] + received[step].astype(F32)).astype(BF16) for step in range(NX)]
    partial, *summed = lax.optimization_barrier((partial, *summed))
    grad_heads = lax.all_to_all(partial, "y", 0, 0, tiled=True)
    spread = [summed[0]] + [shifted(summed[step], "x", NX, step) for step in range(1, NX)]
    by_zone = sum(entry.astype(F32) for entry in spread).astype(BF16)
    last = [cross(by_zone[shift], shift) for shift in range(NZ)]
    grad_weight = sum(entry.astype(F32) for entry in last).astype(BF16)

    grad_query, grad_key, grad_value = call(
        backward_kernel,
        (shape((TOK, DH), BF16),) * 3,
        5 * 2 * IMAGES * PATCH * PATCH * DH,
        2 << 20,
        (query_input, key_input, value_input, query_gain, key_gain, attention, grad_heads),
    )
    return grad_query, grad_key, grad_value, grad_weight


def solution(mesh):
    axes = ("zh", "x", "core", "y", "zl")
    fine = Mesh(mesh.devices.reshape(NZ, NX, NC, NY, NL), axes)
    tokens, heads = ("zh", "x", "core"), ("y", "zl")
    in_specs = (
        P(tokens, heads),
        P(tokens, heads),
        P(tokens, heads),
        P(),
        P(),
        P(heads, tokens),
        P(tokens + heads, None),
    )
    out_specs = (P(tokens, heads), P(tokens, heads), P(tokens, heads), P(heads, tokens))
    return jax.shard_map(shards, mesh=fine, in_specs=in_specs, out_specs=out_specs, check_vma=False)
```

```python
import functools
import math

import jax
import jax.numpy as jnp
from jax import lax
from jax.experimental import pallas as pl
from jax.experimental.pallas import tpu as pltpu
from jax.sharding import Mesh
from jax.sharding import PartitionSpec as P

DH = 128
PATCH = 256
IMAGES = 2
TOK = 512
NZ, NX, NC, NY, NL = 3, 4, 2, 8, 4
BLK = 256
WIDE = NZ * BLK
epsilon = 1e-06
F32 = jnp.float32
BF16 = jnp.bfloat16
VMEM_LIMIT = 32 * 1024 * 1024
SCALING = 1.0 / math.sqrt(DH)


def dot(a, b, ca, cb):
    return lax.dot_general(a, b, (((ca,), (cb,)), ((), ())), preferred_element_type=F32)


def normalize(inputs):
    inputs = inputs.astype(F32)
    average = jnp.mean(inputs, axis=-1, keepdims=True)
    centred = inputs - average
    inverse = lax.rsqrt(jnp.mean(centred * centred, axis=-1, keepdims=True) + epsilon)
    return centred * inverse, inverse


def norm_back(gradient, unit_rows, inverse, gain):
    scaled = gradient * gain
    return (
        scaled
        - jnp.mean(scaled, axis=-1, keepdims=True)
        - unit_rows * jnp.mean(scaled * unit_rows, axis=-1, keepdims=True)
    ) * inverse


def cut_kernel(go_ref, cut_ref):
    for zone in range(NZ):
        for low in range(NL):
            for core in range(NC):
                source = ((zone * NL + low) * NC + core) * BLK
                piece = go_ref[:, source : source + BLK]
                cut_ref[core * NL + low, :, zone * BLK : (zone + 1) * BLK] = piece


def forward_kernel(q_ref, k_ref, v_ref, qg_ref, kg_ref, mixed_ref, att_ref):
    for image in range(IMAGES):
        rows = pl.ds(image * PATCH, PATCH)
        query_low = (normalize(q_ref[rows, :])[0] * qg_ref[...]).astype(BF16)
        key_low = (normalize(k_ref[rows, :])[0] * kg_ref[...]).astype(BF16)
        exponent = jnp.exp(dot(query_low, key_low, 1, 1) * SCALING)
        attention = exponent / jnp.sum(exponent, axis=-1, keepdims=True)
        att_ref[image] = attention
        mixed = dot(v_ref[rows, :], attention.astype(BF16), 0, 1)
        mixed_ref[:, rows] = mixed.astype(BF16)


def backward_kernel(
    q_ref, k_ref, v_ref, qg_ref, kg_ref, att_ref, gh_ref, dq_ref, dk_ref, dv_ref
):
    for image in range(IMAGES):
        rows = pl.ds(image * PATCH, PATCH)
        total = gh_ref[0, rows, :].astype(F32)
        for part in range(1, NL):
            total = total + gh_ref[part, rows, :].astype(F32)
        grad_heads = total.astype(BF16)
        query_unit, query_inv = normalize(q_ref[rows, :])
        key_unit, key_inv = normalize(k_ref[rows, :])
        query_low = (query_unit * qg_ref[...]).astype(BF16)
        key_low = (key_unit * kg_ref[...]).astype(BF16)
        attention = att_ref[image]
        dv_ref[rows, :] = dot(attention.astype(BF16), grad_heads, 0, 0).astype(BF16)
        grad_attention = dot(grad_heads, v_ref[rows, :], 1, 1)
        row_delta = jnp.sum(attention * grad_attention, axis=-1, keepdims=True)
        grad_scores = (attention * (grad_attention - row_delta)).astype(BF16)
        grad_qn = dot(grad_scores, key_low, 1, 0) * SCALING
        grad_kn = dot(grad_scores, query_low, 0, 0) * SCALING
        dq_ref[rows, :] = norm_back(grad_qn, query_unit, query_inv, qg_ref[...]).astype(BF16)
        dk_ref[rows, :] = norm_back(grad_kn, key_unit, key_inv, kg_ref[...]).astype(BF16)


def block(ref, side, zone):
    columns = pl.ds(zone * BLK, BLK)
    return ref[:, pl.ds(side * NL, NL), :, columns].reshape(TOK, BLK)


def heads_kernel(g_ref, own_ref, keep_ref, send_ref):
    here, core = lax.axis_index("zh"), lax.axis_index("core")
    for ref, side in ((send_ref, 1 - core), (keep_ref, core)):
        total = None
        for step in range(NZ):
            rows = block(g_ref, side, lax.rem(here + NZ - step, NZ))
            term = dot(rows, own_ref[:, step].reshape(NL * DH, BLK), 1, 1)
            total = term if total is None else total + term
        for head in range(NL):
            ref[head] = total[:, head * DH : (head + 1) * DH].astype(ref.dtype)


def weight_kernel(g_ref, own_ref, other_ref, out_ref):
    here, core = lax.axis_index("zh"), lax.axis_index("core")
    own = own_ref[...].reshape(NL * DH, TOK)
    other = other_ref[...].reshape(NL * DH, TOK)
    for step in range(NZ):
        zone = lax.rem(here + step, NZ)
        total = dot(own, block(g_ref, core, zone), 1, 0)
        total = total + dot(other, block(g_ref, 1 - core, zone), 1, 0)
        out_ref[:, step] = total.reshape(NL, DH, BLK).astype(BF16)


def call(kernel, outs, flops, moved, operands):
    return pl.pallas_call(
        kernel,
        out_shape=outs,
        in_specs=[pl.BlockSpec(memory_space=pltpu.VMEM)] * len(operands),
        out_specs=jax.tree.map(lambda _: pl.BlockSpec(memory_space=pltpu.VMEM), outs),
        compiler_params=pltpu.CompilerParams(vmem_limit_bytes=VMEM_LIMIT),
        cost_estimate=pl.CostEstimate(flops=flops, bytes_accessed=moved, transcendentals=0),
    )(*operands)


def cross(entry, shift):
    pairs = []
    for zone in range(NZ):
        for across in range(NX):
            for low in range(NL):
                target = (zone + shift) % NZ
                pairs.append(
                    ((zone * NX + across) * NL + low, (target * NX + low) * NL + across)
                )
    return lax.ppermute(entry, ("zh", "x", "zl"), pairs)


def share(entry, axis, size):
    copies = jnp.broadcast_to(entry[None], (size,) + entry.shape)
    return lax.all_to_all(copies, axis, 0, 0, tiled=True)


def swap_cores(entry):
    return lax.ppermute(entry, "core", [(0, 1), (1, 0)])


def shards(query_input, key_input, value_input, query_gain, key_gain, out_weight, grad_output):
    query_gain = query_gain.reshape(1, DH)
    key_gain = key_gain.reshape(1, DH)
    shape = jax.ShapeDtypeStruct

    rows = grad_output.shape[0]
    groups = NC * NL
    pieces = call(cut_kernel, shape((groups, rows, WIDE), BF16), 0, 1 << 18, (grad_output,))
    exchanged = lax.all_to_all(pieces, ("core", "zl"), 0, 0, tiled=True)
    gathered = lax.all_gather(exchanged, "y", axis=0)

    mixed, attention = call(
        forward_kernel,
        (shape((DH, TOK), BF16), shape((IMAGES, PATCH, PATCH), F32)),
        2 * 2 * IMAGES * PATCH * PATCH * DH,
        1 << 20,
        (query_input, key_input, value_input, query_gain, key_gain),
    )
    exchanged, out_weight, mixed = lax.optimization_barrier((exchanged, out_weight, mixed))
    mixed_own = share(mixed, "zl", NL)
    moved = [cross(out_weight, shift) for shift in range(NZ)]
    mixed_own, *moved = lax.optimization_barrier((mixed_own, *moved))
    moved = jnp.stack(moved)
    mixed_other = swap_cores(mixed_own)
    own = lax.all_gather(moved, "x", axis=0)
    gathered, mixed_own, mixed_other, own = lax.optimization_barrier(
        (gathered, mixed_own, mixed_other, own)
    )

    partial = call(
        weight_kernel,
        shape((NL, NZ, DH, BLK), BF16),
        2 * TOK * NY * DH * WIDE,
        5 << 20,
        (gathered, mixed_own, mixed_other),
    )
    spread = lax.all_to_all(partial, "x", 0, 0, tiled=True)

    half = (NL, TOK, DH)
    keep, send = call(
        heads_kernel,
        (shape(half, F32), shape(half, BF16)),
        2 * TOK * NY * DH * WIDE,
        4 << 20,
        (gathered, own),
    )
    received = swap_cores(send)
    summed = (keep + received.astype(F32)).astype(BF16)
    grad_heads = lax.all_to_all(summed, "zl", 0, 0, tiled=True)

    by_zone = sum(spread[part].astype(F32) for part in range(NX)).astype(BF16)
    last = [cross(by_zone[shift], shift) for shift in range(NZ)]
    grad_weight = sum(entry.astype(F32) for entry in last).astype(BF16)

    grad_query, grad_key, grad_value = call(
        backward_kernel,
        (shape((TOK, DH), BF16),) * 3,
        5 * 2 * IMAGES * PATCH * PATCH * DH,
        2 << 20,
        (query_input, key_input, value_input, query_gain, key_gain, attention, grad_heads),
    )
    return grad_query, grad_key, grad_value, grad_weight


def solution(mesh):
    axes = ("zh", "x", "core", "y", "zl")
    fine = Mesh(mesh.devices.reshape(NZ, NX, NC, NY, NL), axes)
    tokens, heads = ("zh", "x", "core"), ("y", "zl")
    in_specs = (
        P(tokens, heads),
        P(tokens, heads),
        P(tokens, heads),
        P(),
        P(),
        P(heads, tokens),
        P(tokens + heads, None),
    )
    out_specs = (P(tokens, heads), P(tokens, heads), P(tokens, heads), P(heads, tokens))
    return jax.shard_map(shards, mesh=fine, in_specs=in_specs, out_specs=out_specs, check_vma=False)
```

```python
import functools
import math

import jax
import jax.numpy as jnp
from jax import lax
from jax.experimental import pallas as pl
from jax.experimental.pallas import tpu as pltpu
from jax.sharding import Mesh
from jax.sharding import PartitionSpec as P

DH = 128
PATCH = 256
IMAGES = 2
TOK = 512
NZ, NX, NC, NY, NL = 3, 4, 2, 8, 4
BLK = 256
WIDE = NZ * BLK
epsilon = 1e-06
F32 = jnp.float32
BF16 = jnp.bfloat16
VMEM_LIMIT = 32 * 1024 * 1024
SCALING = 1.0 / math.sqrt(DH)


def dot(a, b, ca, cb):
    return lax.dot_general(a, b, (((ca,), (cb,)), ((), ())), preferred_element_type=F32)


def normalize(inputs):
    inputs = inputs.astype(F32)
    average = jnp.mean(inputs, axis=-1, keepdims=True)
    centred = inputs - average
    inverse = lax.rsqrt(jnp.mean(centred * centred, axis=-1, keepdims=True) + epsilon)
    return centred * inverse, inverse


def norm_back(gradient, unit_rows, inverse, gain):
    scaled = gradient * gain
    return (
        scaled
        - jnp.mean(scaled, axis=-1, keepdims=True)
        - unit_rows * jnp.mean(scaled * unit_rows, axis=-1, keepdims=True)
    ) * inverse


def cut_kernel(go_ref, cut_ref):
    for zone in range(NZ):
        for low in range(NL):
            for core in range(NC):
                source = ((zone * NL + low) * NC + core) * BLK
                piece = go_ref[:, source : source + BLK]
                cut_ref[core * NL + low, :, zone * BLK : (zone + 1) * BLK] = piece


def forward_kernel(q_ref, k_ref, v_ref, qg_ref, kg_ref, mixed_ref, att_ref):
    for image in range(IMAGES):
        rows = pl.ds(image * PATCH, PATCH)
        query_low = (normalize(q_ref[rows, :])[0] * qg_ref[...]).astype(BF16)
        key_low = (normalize(k_ref[rows, :])[0] * kg_ref[...]).astype(BF16)
        exponent = jnp.exp(dot(query_low, key_low, 1, 1) * SCALING)
        attention = exponent / jnp.sum(exponent, axis=-1, keepdims=True)
        att_ref[image] = attention
        mixed = dot(v_ref[rows, :], attention.astype(BF16), 0, 1)
        mixed_ref[:, rows] = mixed.astype(BF16)


def backward_kernel(
    q_ref, k_ref, v_ref, qg_ref, kg_ref, att_ref, *refs
):
    gh_refs, (dq_ref, dk_ref, dv_ref) = refs[:NL], refs[NL:]
    for image in range(IMAGES):
        rows = pl.ds(image * PATCH, PATCH)
        total = gh_refs[0][rows, :].astype(F32)
        for part in range(1, NL):
            total = total + gh_refs[part][rows, :].astype(F32)
        grad_heads = total.astype(BF16)
        query_unit, query_inv = normalize(q_ref[rows, :])
        key_unit, key_inv = normalize(k_ref[rows, :])
        query_low = (query_unit * qg_ref[...]).astype(BF16)
        key_low = (key_unit * kg_ref[...]).astype(BF16)
        attention = att_ref[image]
        dv_ref[rows, :] = dot(attention.astype(BF16), grad_heads, 0, 0).astype(BF16)
        grad_attention = dot(grad_heads, v_ref[rows, :], 1, 1)
        row_delta = jnp.sum(attention * grad_attention, axis=-1, keepdims=True)
        grad_scores = (attention * (grad_attention - row_delta)).astype(BF16)
        grad_qn = dot(grad_scores, key_low, 1, 0) * SCALING
        grad_kn = dot(grad_scores, query_low, 0, 0) * SCALING
        dq_ref[rows, :] = norm_back(grad_qn, query_unit, query_inv, qg_ref[...]).astype(BF16)
        dk_ref[rows, :] = norm_back(grad_kn, key_unit, key_inv, kg_ref[...]).astype(BF16)


def block(ref, side, zone):
    columns = slice(zone * BLK, (zone + 1) * BLK)
    return ref[:, pl.ds(side * NL, NL), :, columns].reshape(TOK, BLK)


def heads_kernel(g_ref, own_ref, keep_ref, send_ref):
    core, low = lax.axis_index("core"), lax.axis_index("zl")
    for ref, side in ((send_ref, 1 - core), (keep_ref, core)):
        total = None
        for zone in range(NZ):
            weight = jnp.concatenate([own_ref[zone, low ^ step] for step in range(NL)], axis=0)
            term = dot(block(g_ref, side, zone), weight, 1, 1)
            total = term if total is None else total + term
        for step in range(NL):
            ref[step] = total[:, step * DH : (step + 1) * DH].astype(ref.dtype)


def weight_kernel(g_ref, own_ref, other_ref, out_ref):
    core = lax.axis_index("core")
    own = own_ref[...].reshape(NL * DH, TOK)
    other = other_ref[...].reshape(NL * DH, TOK)
    for zone in range(NZ):
        total = dot(own, block(g_ref, core, zone), 1, 0)
        total = total + dot(other, block(g_ref, 1 - core, zone), 1, 0)
        out_ref[zone] = total.reshape(NL, DH, BLK).astype(BF16)


def call(kernel, outs, flops, moved, operands):
    return pl.pallas_call(
        kernel,
        out_shape=outs,
        in_specs=[pl.BlockSpec(memory_space=pltpu.VMEM)] * len(operands),
        out_specs=jax.tree.map(lambda _: pl.BlockSpec(memory_space=pltpu.VMEM), outs),
        compiler_params=pltpu.CompilerParams(vmem_limit_bytes=VMEM_LIMIT),
        cost_estimate=pl.CostEstimate(flops=flops, bytes_accessed=moved, transcendentals=0),
    )(*operands)


def cross(entry):
    pairs = [(at * NL + low, low * NL + at) for at in range(NX) for low in range(NL)]
    return lax.ppermute(entry, ("x", "zl"), pairs)


def flip(entry, step):
    return lax.ppermute(entry, "zl", [(at, at ^ step) for at in range(NL)])


def swap_cores(entry):
    return lax.ppermute(entry, "core", [(0, 1), (1, 0)])


def shards(query_input, key_input, value_input, query_gain, key_gain, out_weight, grad_output):
    query_gain = query_gain.reshape(1, DH)
    key_gain = key_gain.reshape(1, DH)
    shape = jax.ShapeDtypeStruct

    rows = grad_output.shape[0]
    groups = NC * NL
    pieces = call(cut_kernel, shape((groups, rows, WIDE), BF16), 0, 1 << 18, (grad_output,))
    exchanged = lax.all_to_all(pieces, ("core", "zl"), 0, 0, tiled=True)
    gathered = lax.all_gather(exchanged, "y", axis=0)

    mixed, attention = call(
        forward_kernel,
        (shape((DH, TOK), BF16), shape((IMAGES, PATCH, PATCH), F32)),
        2 * 2 * IMAGES * PATCH * PATCH * DH,
        1 << 20,
        (query_input, key_input, value_input, query_gain, key_gain),
    )
    exchanged, out_weight, mixed = lax.optimization_barrier((exchanged, out_weight, mixed))
    zones = NZ * NX
    crossed = cross(out_weight)
    copies = jnp.broadcast_to(crossed[None], (zones, DH, BLK))
    own = lax.all_to_all(copies, ("zh", "x"), 0, 0, tiled=True).reshape(NZ, NX, DH, BLK)
    mixed_own = lax.all_gather(mixed, "zl", axis=0)
    mixed_other = swap_cores(mixed_own)
    gathered, mixed_own, mixed_other, own = lax.optimization_barrier(
        (gathered, mixed_own, mixed_other, own)
    )

    partial = call(
        weight_kernel,
        shape((NZ, NX, DH, BLK), BF16),
        2 * TOK * NY * DH * WIDE,
        5 << 20,
        (gathered, mixed_own, mixed_other),
    )
    spread = lax.all_to_all(partial.reshape(zones, DH, BLK), ("zh", "x"), 0, 0, tiled=True)

    half = (NL, TOK, DH)
    keep, send = call(
        heads_kernel,
        (shape(half, F32), shape(half, BF16)),
        2 * TOK * NY * DH * WIDE,
        4 << 20,
        (gathered, own),
    )
    received = swap_cores(send)
    summed = [(keep[step] + received[step].astype(F32)).astype(BF16) for step in range(NL)]
    grad_heads = [summed[0]] + [flip(summed[step], step) for step in range(1, NL)]

    grad_weight = cross(sum(spread[part].astype(F32) for part in range(zones)).astype(BF16))

    grad_query, grad_key, grad_value = call(
        backward_kernel,
        (shape((TOK, DH), BF16),) * 3,
        5 * 2 * IMAGES * PATCH * PATCH * DH,
        2 << 20,
        (query_input, key_input, value_input, query_gain, key_gain, attention, *grad_heads),
    )
    return grad_query, grad_key, grad_value, grad_weight


def solution(mesh):
    axes = ("zh", "x", "core", "y", "zl")
    fine = Mesh(mesh.devices.reshape(NZ, NX, NC, NY, NL), axes)
    tokens, heads = ("zh", "x", "core"), ("y", "zl")
    in_specs = (
        P(tokens, heads),
        P(tokens, heads),
        P(tokens, heads),
        P(),
        P(),
        P(heads, tokens),
        P(tokens + heads, None),
    )
    out_specs = (P(tokens, heads), P(tokens, heads), P(tokens, heads), P(heads, tokens))
    return jax.shard_map(shards, mesh=fine, in_specs=in_specs, out_specs=out_specs, check_vma=False)
```

```python
import functools
import math

import jax
import jax.numpy as jnp
from jax import lax
from jax.experimental import pallas as pl
from jax.experimental.pallas import tpu as pltpu
from jax.sharding import Mesh
from jax.sharding import PartitionSpec as P

DH = 128
PATCH = 256
IMAGES = 2
TOK = 512
NZ, NX, NC, NY, NL = 3, 4, 2, 8, 4
BLK = 256
WIDE = NZ * BLK
epsilon = 1e-06
F32 = jnp.float32
BF16 = jnp.bfloat16
VMEM_LIMIT = 32 * 1024 * 1024
SCALING = 1.0 / math.sqrt(DH)


def dot(a, b, ca, cb):
    return lax.dot_general(a, b, (((ca,), (cb,)), ((), ())), preferred_element_type=F32)


def normalize(inputs):
    inputs = inputs.astype(F32)
    average = jnp.mean(inputs, axis=-1, keepdims=True)
    centred = inputs - average
    inverse = lax.rsqrt(jnp.mean(centred * centred, axis=-1, keepdims=True) + epsilon)
    return centred * inverse, inverse


def norm_back(gradient, unit_rows, inverse, gain):
    scaled = gradient * gain
    return (
        scaled
        - jnp.mean(scaled, axis=-1, keepdims=True)
        - unit_rows * jnp.mean(scaled * unit_rows, axis=-1, keepdims=True)
    ) * inverse


def cut_kernel(go_ref, cut_ref):
    for zone in range(NZ):
        for low in range(NL):
            for core in range(NC):
                source = ((zone * NL + low) * NC + core) * BLK
                piece = go_ref[:, source : source + BLK]
                cut_ref[core * NL + low, :, zone * BLK : (zone + 1) * BLK] = piece


def forward_kernel(q_ref, k_ref, v_ref, qg_ref, kg_ref, mixed_ref, att_ref):
    for image in range(IMAGES):
        rows = pl.ds(image * PATCH, PATCH)
        query_low = (normalize(q_ref[rows, :])[0] * qg_ref[...]).astype(BF16)
        key_low = (normalize(k_ref[rows, :])[0] * kg_ref[...]).astype(BF16)
        exponent = jnp.exp(dot(query_low, key_low, 1, 1) * SCALING)
        attention = exponent / jnp.sum(exponent, axis=-1, keepdims=True)
        att_ref[image] = attention
        mixed = dot(v_ref[rows, :], attention.astype(BF16), 0, 1)
        mixed_ref[:, rows] = mixed.astype(BF16)


def backward_kernel(
    q_ref, k_ref, v_ref, qg_ref, kg_ref, att_ref, *refs
):
    gh_refs, (dq_ref, dk_ref, dv_ref) = refs[:NL], refs[NL:]
    for image in range(IMAGES):
        rows = pl.ds(image * PATCH, PATCH)
        total = gh_refs[0][rows, :].astype(F32)
        for part in range(1, NL):
            total = total + gh_refs[part][rows, :].astype(F32)
        grad_heads = total.astype(BF16)
        query_unit, query_inv = normalize(q_ref[rows, :])
        key_unit, key_inv = normalize(k_ref[rows, :])
        query_low = (query_unit * qg_ref[...]).astype(BF16)
        key_low = (key_unit * kg_ref[...]).astype(BF16)
        attention = att_ref[image]
        dv_ref[rows, :] = dot(attention.astype(BF16), grad_heads, 0, 0).astype(BF16)
        grad_attention = dot(grad_heads, v_ref[rows, :], 1, 1)
        row_delta = jnp.sum(attention * grad_attention, axis=-1, keepdims=True)
        grad_scores = (attention * (grad_attention - row_delta)).astype(BF16)
        grad_qn = dot(grad_scores, key_low, 1, 0) * SCALING
        grad_kn = dot(grad_scores, query_low, 0, 0) * SCALING
        dq_ref[rows, :] = norm_back(grad_qn, query_unit, query_inv, qg_ref[...]).astype(BF16)
        dk_ref[rows, :] = norm_back(grad_kn, key_unit, key_inv, kg_ref[...]).astype(BF16)


def block(ref, side, zone):
    columns = pl.ds(zone * BLK, BLK)
    return ref[:, pl.ds(side * NL, NL), :, columns].reshape(TOK, BLK)


def heads_kernel(g_ref, own_ref, keep_ref, send_ref):
    core, low = lax.axis_index("core"), lax.axis_index("zl")
    for ref, side in ((send_ref, 1 - core), (keep_ref, core)):
        total = None
        for zone in range(NZ):
            weight = jnp.concatenate([own_ref[zone, low ^ step] for step in range(NL)], axis=0)
            term = dot(block(g_ref, side, zone), weight, 1, 1)
            total = term if total is None else total + term
        for step in range(NL):
            ref[step] = total[:, step * DH : (step + 1) * DH].astype(ref.dtype)


def weight_kernel(g_ref, own_ref, other_ref, out_ref):
    here, core, low = (lax.axis_index(name) for name in ("zh", "core", "zl"))
    own, other = (
        jnp.concatenate([ref[low ^ head] for head in range(NL)], axis=0)
        for ref in (own_ref, other_ref)
    )
    for step in range(NZ):
        zone = lax.rem(here + step, NZ)
        total = dot(own, block(g_ref, core, zone), 1, 0)
        total = total + dot(other, block(g_ref, 1 - core, zone), 1, 0)
        out_ref[:, step] = total.reshape(NL, DH, BLK).astype(BF16)


def call(kernel, outs, flops, moved, operands):
    return pl.pallas_call(
        kernel,
        out_shape=outs,
        in_specs=[pl.BlockSpec(memory_space=pltpu.VMEM)] * len(operands),
        out_specs=jax.tree.map(lambda _: pl.BlockSpec(memory_space=pltpu.VMEM), outs),
        compiler_params=pltpu.CompilerParams(vmem_limit_bytes=VMEM_LIMIT),
        cost_estimate=pl.CostEstimate(flops=flops, bytes_accessed=moved, transcendentals=0),
    )(*operands)


def cross(entry, shift):
    pairs = []
    for zone in range(NZ):
        for across in range(NX):
            for low in range(NL):
                target = (zone + shift) % NZ
                pairs.append(
                    ((zone * NX + across) * NL + low, (target * NX + low) * NL + across)
                )
    return lax.ppermute(entry, ("zh", "x", "zl"), pairs)


def flip(entry, step):
    return lax.ppermute(entry, "zl", [(at, at ^ step) for at in range(NL)])


def swap_cores(entry):
    return lax.ppermute(entry, "core", [(0, 1), (1, 0)])


def shards(query_input, key_input, value_input, query_gain, key_gain, out_weight, grad_output):
    query_gain = query_gain.reshape(1, DH)
    key_gain = key_gain.reshape(1, DH)
    shape = jax.ShapeDtypeStruct

    rows = grad_output.shape[0]
    groups = NC * NL
    pieces = call(cut_kernel, shape((groups, rows, WIDE), BF16), 0, 1 << 18, (grad_output,))
    exchanged = lax.all_to_all(pieces, ("core", "zl"), 0, 0, tiled=True)
    gathered = lax.all_gather(exchanged, "y", axis=0)

    exchanged, out_weight = lax.optimization_barrier((exchanged, out_weight))
    zones = NZ * NX
    crossed = cross(out_weight, 0)
    query_input, crossed = lax.optimization_barrier((query_input, crossed))
    copies = jnp.broadcast_to(crossed[None], (zones, DH, BLK))
    own = lax.all_to_all(copies, ("zh", "x"), 0, 0, tiled=True).reshape(NZ, NX, DH, BLK)
    mixed, attention = call(
        forward_kernel,
        (shape((DH, TOK), BF16), shape((IMAGES, PATCH, PATCH), F32)),
        2 * 2 * IMAGES * PATCH * PATCH * DH,
        1 << 20,
        (query_input, key_input, value_input, query_gain, key_gain),
    )
    mixed_own = jnp.stack([mixed] + [flip(mixed, step) for step in range(1, NL)])
    mixed_other = swap_cores(mixed_own)
    gathered, mixed_own, mixed_other, own = lax.optimization_barrier(
        (gathered, mixed_own, mixed_other, own)
    )

    half = (NL, TOK, DH)
    keep, send = call(
        heads_kernel,
        (shape(half, F32), shape(half, BF16)),
        2 * TOK * NY * DH * WIDE,
        4 << 20,
        (gathered, own),
    )
    gathered, send = lax.optimization_barrier((gathered, send))
    partial = call(
        weight_kernel,
        shape((NL, NZ, DH, BLK), BF16),
        2 * TOK * NY * DH * WIDE,
        5 << 20,
        (gathered, mixed_own, mixed_other),
    )
    spread = lax.all_to_all(partial, "x", 0, 0, tiled=True)
    received = swap_cores(send)
    summed = [(keep[step] + received[step].astype(F32)).astype(BF16) for step in range(NL)]
    grad_heads = [summed[0]] + [flip(summed[step], step) for step in range(1, NL)]

    spread, *grad_heads = lax.optimization_barrier((spread, *grad_heads))
    by_zone = sum(spread[part].astype(F32) for part in range(NX)).astype(BF16)
    last = [cross(by_zone[shift], shift) for shift in range(NZ)]
    grad_weight = sum(entry.astype(F32) for entry in last).astype(BF16)

    grad_query, grad_key, grad_value = call(
        backward_kernel,
        (shape((TOK, DH), BF16),) * 3,
        5 * 2 * IMAGES * PATCH * PATCH * DH,
        2 << 20,
        (query_input, key_input, value_input, query_gain, key_gain, attention, *grad_heads),
    )
    return grad_query, grad_key, grad_value, grad_weight


def solution(mesh):
    axes = ("zh", "x", "core", "y", "zl")
    fine = Mesh(mesh.devices.reshape(NZ, NX, NC, NY, NL), axes)
    tokens, heads = ("zh", "x", "core"), ("y", "zl")
    in_specs = (
        P(tokens, heads),
        P(tokens, heads),
        P(tokens, heads),
        P(),
        P(),
        P(heads, tokens),
        P(tokens + heads, None),
    )
    out_specs = (P(tokens, heads), P(tokens, heads), P(tokens, heads), P(heads, tokens))
    return jax.shard_map(shards, mesh=fine, in_specs=in_specs, out_specs=out_specs, check_vma=False)
```

```python
import functools
import math

import jax
import jax.numpy as jnp
from jax import lax
from jax.experimental import pallas as pl
from jax.experimental.pallas import tpu as pltpu
from jax.sharding import Mesh
from jax.sharding import PartitionSpec as P

DH = 128
PATCH = 256
IMAGES = 2
TOK = 512
NZ, NX, NC, NY, NL = 3, 4, 2, 8, 4
BLK = 256
WIDE = NZ * BLK
epsilon = 1e-06
F32 = jnp.float32
BF16 = jnp.bfloat16
VMEM_LIMIT = 32 * 1024 * 1024
SCALING = 1.0 / math.sqrt(DH)


def dot(a, b, ca, cb):
    return lax.dot_general(a, b, (((ca,), (cb,)), ((), ())), preferred_element_type=F32)


def normalize(inputs):
    inputs = inputs.astype(F32)
    average = jnp.mean(inputs, axis=-1, keepdims=True)
    centred = inputs - average
    inverse = lax.rsqrt(jnp.mean(centred * centred, axis=-1, keepdims=True) + epsilon)
    return centred * inverse, inverse


def norm_back(gradient, unit_rows, inverse, gain):
    scaled = gradient * gain
    return (
        scaled
        - jnp.mean(scaled, axis=-1, keepdims=True)
        - unit_rows * jnp.mean(scaled * unit_rows, axis=-1, keepdims=True)
    ) * inverse


def cut_kernel(go_ref, cut_ref):
    for zone in range(NZ):
        for low in range(NL):
            for core in range(NC):
                source = ((zone * NL + low) * NC + core) * BLK
                piece = go_ref[:, source : source + BLK]
                cut_ref[core * NL + low, :, zone * BLK : (zone + 1) * BLK] = piece


def forward_kernel(q_ref, k_ref, v_ref, qg_ref, kg_ref, mixed_ref, att_ref):
    for image in range(IMAGES):
        rows = pl.ds(image * PATCH, PATCH)
        query_low = (normalize(q_ref[rows, :])[0] * qg_ref[...]).astype(BF16)
        key_low = (normalize(k_ref[rows, :])[0] * kg_ref[...]).astype(BF16)
        exponent = jnp.exp(dot(query_low, key_low, 1, 1) * SCALING)
        attention = exponent / jnp.sum(exponent, axis=-1, keepdims=True)
        att_ref[image] = attention
        mixed = dot(v_ref[rows, :], attention.astype(BF16), 0, 1)
        mixed_ref[:, rows] = mixed.astype(BF16)


def backward_kernel(
    q_ref, k_ref, v_ref, qg_ref, kg_ref, att_ref, gh_ref, dq_ref, dk_ref, dv_ref
):
    for image in range(IMAGES):
        rows = pl.ds(image * PATCH, PATCH)
        grad_heads = gh_ref[rows, :]
        query_unit, query_inv = normalize(q_ref[rows, :])
        key_unit, key_inv = normalize(k_ref[rows, :])
        query_low = (query_unit * qg_ref[...]).astype(BF16)
        key_low = (key_unit * kg_ref[...]).astype(BF16)
        attention = att_ref[image]
        dv_ref[rows, :] = dot(attention.astype(BF16), grad_heads, 0, 0).astype(BF16)
        grad_attention = dot(grad_heads, v_ref[rows, :], 1, 1)
        row_delta = jnp.sum(attention * grad_attention, axis=-1, keepdims=True)
        grad_scores = (attention * (grad_attention - row_delta)).astype(BF16)
        grad_qn = dot(grad_scores, key_low, 1, 0) * SCALING
        grad_kn = dot(grad_scores, query_low, 0, 0) * SCALING
        dq_ref[rows, :] = norm_back(grad_qn, query_unit, query_inv, qg_ref[...]).astype(BF16)
        dk_ref[rows, :] = norm_back(grad_kn, key_unit, key_inv, kg_ref[...]).astype(BF16)


def block(ref, side, zone):
    columns = pl.ds(zone * BLK, BLK)
    return ref[:, pl.ds(side * NL, NL), :, columns].reshape(TOK, BLK)


def heads_kernel(g_ref, own_ref, out_ref):
    here = lax.axis_index("zh")
    for side in range(NC):
        total = None
        for step in range(NZ):
            rows = block(g_ref, side, lax.rem(here + NZ - step, NZ))
            term = dot(rows, own_ref[:, step].reshape(NL * DH, BLK), 1, 1)
            total = term if total is None else total + term
        for head in range(NL):
            out_ref[side * NL + head] = total[:, head * DH : (head + 1) * DH].astype(BF16)


def weight_kernel(g_ref, own_ref, other_ref, out_ref):
    here, core = lax.axis_index("zh"), lax.axis_index("core")
    own = own_ref[...].reshape(NL * DH, TOK)
    other = other_ref[...].reshape(NL * DH, TOK)
    for step in range(NZ):
        zone = lax.rem(here + step, NZ)
        total = dot(own, block(g_ref, core, zone), 1, 0)
        total = total + dot(other, block(g_ref, 1 - core, zone), 1, 0)
        out_ref[:, step] = total.reshape(NL, DH, BLK).astype(BF16)


def call(kernel, outs, flops, moved, operands):
    return pl.pallas_call(
        kernel,
        out_shape=outs,
        in_specs=[pl.BlockSpec(memory_space=pltpu.VMEM)] * len(operands),
        out_specs=jax.tree.map(lambda _: pl.BlockSpec(memory_space=pltpu.VMEM), outs),
        compiler_params=pltpu.CompilerParams(vmem_limit_bytes=VMEM_LIMIT),
        cost_estimate=pl.CostEstimate(flops=flops, bytes_accessed=moved, transcendentals=0),
    )(*operands)


def cross(entry, shift):
    pairs = []
    for zone in range(NZ):
        for across in range(NX):
            for low in range(NL):
                target = (zone + shift) % NZ
                pairs.append(
                    ((zone * NX + across) * NL + low, (target * NX + low) * NL + across)
                )
    return lax.ppermute(entry, ("zh", "x", "zl"), pairs)


def share(entry, axis, size):
    copies = jnp.broadcast_to(entry[None], (size,) + entry.shape)
    return lax.all_to_all(copies, axis, 0, 0, tiled=True)


def swap_cores(entry):
    return lax.ppermute(entry, "core", [(0, 1), (1, 0)])


def shards(query_input, key_input, value_input, query_gain, key_gain, out_weight, grad_output):
    query_gain = query_gain.reshape(1, DH)
    key_gain = key_gain.reshape(1, DH)
    shape = jax.ShapeDtypeStruct

    rows = grad_output.shape[0]
    groups = NC * NL
    pieces = call(cut_kernel, shape((groups, rows, WIDE), BF16), 0, 1 << 18, (grad_output,))
    exchanged = lax.all_to_all(pieces, ("core", "zl"), 0, 0, tiled=True)
    gathered = lax.all_gather(exchanged, "y", axis=0)

    mixed, attention = call(
        forward_kernel,
        (shape((DH, TOK), BF16), shape((IMAGES, PATCH, PATCH), F32)),
        2 * 2 * IMAGES * PATCH * PATCH * DH,
        1 << 20,
        (query_input, key_input, value_input, query_gain, key_gain),
    )
    exchanged, out_weight = lax.optimization_barrier((exchanged, out_weight))
    moved = [cross(out_weight, shift) for shift in range(NZ)]
    mixed, *moved = lax.optimization_barrier((mixed, *moved))
    mixed_own = share(mixed, "zl", NL)
    own = lax.all_gather(jnp.stack(moved), "x", axis=0)
    mixed_own, own = lax.optimization_barrier((mixed_own, own))
    mixed_other = swap_cores(mixed_own)
    gathered, own, mixed_other = lax.optimization_barrier((gathered, own, mixed_other))

    heads = call(
        heads_kernel,
        shape((groups, TOK, DH), BF16),
        2 * TOK * NY * DH * WIDE,
        4 << 20,
        (gathered, own),
    )
    gathered, heads = lax.optimization_barrier((gathered, heads))
    grad_heads = lax.psum_scatter(heads, ("core", "zl"), scatter_dimension=0, tiled=True)
    partial = call(
        weight_kernel,
        shape((NL, NZ, DH, BLK), BF16),
        2 * TOK * NY * DH * WIDE,
        5 << 20,
        (gathered, mixed_own, mixed_other),
    )
    spread = lax.all_to_all(partial, "x", 0, 0, tiled=True)
    by_zone = sum(spread[part].astype(F32) for part in range(NX)).astype(BF16)
    last = [cross(by_zone[shift], shift) for shift in range(NZ)]
    grad_weight = sum(entry.astype(F32) for entry in last).astype(BF16)

    grad_query, grad_key, grad_value = call(
        backward_kernel,
        (shape((TOK, DH), BF16),) * 3,
        5 * 2 * IMAGES * PATCH * PATCH * DH,
        2 << 20,
        (query_input, key_input, value_input, query_gain, key_gain, attention, grad_heads.reshape(TOK, DH)),
    )
    return grad_query, grad_key, grad_value, grad_weight


def solution(mesh):
    axes = ("zh", "x", "core", "y", "zl")
    fine = Mesh(mesh.devices.reshape(NZ, NX, NC, NY, NL), axes)
    tokens, heads = ("zh", "x", "core"), ("y", "zl")
    in_specs = (
        P(tokens, heads),
        P(tokens, heads),
        P(tokens, heads),
        P(),
        P(),
        P(heads, tokens),
        P(tokens + heads, None),
    )
    out_specs = (P(tokens, heads), P(tokens, heads), P(tokens, heads), P(heads, tokens))
    return jax.shard_map(shards, mesh=fine, in_specs=in_specs, out_specs=out_specs, check_vma=False)
```

```python
import functools
import math

import jax
import jax.numpy as jnp
from jax import lax
from jax.experimental import pallas as pl
from jax.experimental.pallas import tpu as pltpu
from jax.sharding import Mesh
from jax.sharding import PartitionSpec as P

DH = 128
PATCH = 256
IMAGES = 2
TOK = 512
NZ, NX, NC, NY, NL = 3, 4, 2, 8, 4
BLK = 256
WIDE = NZ * BLK
epsilon = 1e-06
F32 = jnp.float32
BF16 = jnp.bfloat16
VMEM_LIMIT = 12 * 1024 * 1024
SCALING = 1.0 / math.sqrt(DH)


def dot(a, b, ca, cb):
    return lax.dot_general(a, b, (((ca,), (cb,)), ((), ())), preferred_element_type=F32)


def normalize(inputs):
    inputs = inputs.astype(F32)
    average = jnp.mean(inputs, axis=-1, keepdims=True)
    centred = inputs - average
    inverse = lax.rsqrt(jnp.mean(centred * centred, axis=-1, keepdims=True) + epsilon)
    return centred * inverse, inverse


def norm_back(gradient, unit_rows, inverse, gain):
    scaled = gradient * gain
    return (
        scaled
        - jnp.mean(scaled, axis=-1, keepdims=True)
        - unit_rows * jnp.mean(scaled * unit_rows, axis=-1, keepdims=True)
    ) * inverse


def cut_kernel(go_ref, cut_ref):
    for zone in range(NZ):
        for low in range(NL):
            for core in range(NC):
                source = ((zone * NL + low) * NC + core) * BLK
                piece = go_ref[:, source : source + BLK]
                cut_ref[core * NL + low, :, zone * BLK : (zone + 1) * BLK] = piece


def forward_kernel(q_ref, k_ref, v_ref, qg_ref, kg_ref, mixed_ref, att_ref):
    for image in range(IMAGES):
        rows = pl.ds(image * PATCH, PATCH)
        query_low = (normalize(q_ref[rows, :])[0] * qg_ref[...]).astype(BF16)
        key_low = (normalize(k_ref[rows, :])[0] * kg_ref[...]).astype(BF16)
        exponent = jnp.exp(dot(query_low, key_low, 1, 1) * SCALING)
        attention = exponent / jnp.sum(exponent, axis=-1, keepdims=True)
        att_ref[image] = attention
        mixed = dot(v_ref[rows, :], attention.astype(BF16), 0, 1)
        mixed_ref[:, rows] = mixed.astype(BF16)


def backward_kernel(
    q_ref, k_ref, v_ref, qg_ref, kg_ref, att_ref, gh_ref, dq_ref, dk_ref, dv_ref
):
    for image in range(IMAGES):
        rows = pl.ds(image * PATCH, PATCH)
        grad_heads = gh_ref[rows, :]
        query_unit, query_inv = normalize(q_ref[rows, :])
        key_unit, key_inv = normalize(k_ref[rows, :])
        query_low = (query_unit * qg_ref[...]).astype(BF16)
        key_low = (key_unit * kg_ref[...]).astype(BF16)
        attention = att_ref[image]
        dv_ref[rows, :] = dot(attention.astype(BF16), grad_heads, 0, 0).astype(BF16)
        grad_attention = dot(grad_heads, v_ref[rows, :], 1, 1)
        row_delta = jnp.sum(attention * grad_attention, axis=-1, keepdims=True)
        grad_scores = (attention * (grad_attention - row_delta)).astype(BF16)
        grad_qn = dot(grad_scores, key_low, 1, 0) * SCALING
        grad_kn = dot(grad_scores, query_low, 0, 0) * SCALING
        dq_ref[rows, :] = norm_back(grad_qn, query_unit, query_inv, qg_ref[...]).astype(BF16)
        dk_ref[rows, :] = norm_back(grad_kn, key_unit, key_inv, kg_ref[...]).astype(BF16)


def block(ref, side, zone):
    columns = pl.ds(zone * BLK, BLK)
    return ref[:, pl.ds(side * NL, NL), :, columns].reshape(TOK, BLK)


def heads_kernel(g_ref, own_ref, keep_ref, send_ref):
    here, core = lax.axis_index("zh"), lax.axis_index("core")
    for ref, side in ((send_ref, 1 - core), (keep_ref, core)):
        total = None
        for step in range(NZ):
            rows = block(g_ref, side, lax.rem(here + NZ - step, NZ))
            term = dot(rows, own_ref[:, step].reshape(NL * DH, BLK), 1, 1)
            total = term if total is None else total + term
        for head in range(NL):
            ref[head] = total[:, head * DH : (head + 1) * DH].astype(BF16)


def weight_kernel(g_ref, own_ref, other_ref, out_ref):
    here, core = lax.axis_index("zh"), lax.axis_index("core")
    own = own_ref[...].reshape(NL * DH, TOK)
    other = other_ref[...].reshape(NL * DH, TOK)
    for step in range(NZ):
        zone = lax.rem(here + step, NZ)
        total = dot(own, block(g_ref, core, zone), 1, 0)
        total = total + dot(other, block(g_ref, 1 - core, zone), 1, 0)
        out_ref[:, step] = total.reshape(NL, DH, BLK).astype(BF16)


def call(kernel, outs, flops, moved, operands):
    return pl.pallas_call(
        kernel,
        out_shape=outs,
        in_specs=[pl.BlockSpec(memory_space=pltpu.VMEM)] * len(operands),
        out_specs=jax.tree.map(lambda _: pl.BlockSpec(memory_space=pltpu.VMEM), outs),
        compiler_params=pltpu.CompilerParams(vmem_limit_bytes=VMEM_LIMIT),
        cost_estimate=pl.CostEstimate(flops=flops, bytes_accessed=moved, transcendentals=0),
    )(*operands)


def cross(entry, shift):
    pairs = []
    for zone in range(NZ):
        for across in range(NX):
            for low in range(NL):
                target = (zone + shift) % NZ
                pairs.append(
                    ((zone * NX + across) * NL + low, (target * NX + low) * NL + across)
                )
    return lax.ppermute(entry, ("zh", "x", "zl"), pairs)


def share(entry, axis, size):
    copies = jnp.broadcast_to(entry[None], (size,) + entry.shape)
    return lax.all_to_all(copies, axis, 0, 0, tiled=True)


def swap_cores(entry):
    return lax.ppermute(entry, "core", [(0, 1), (1, 0)])


def shards(query_input, key_input, value_input, query_gain, key_gain, out_weight, grad_output):
    query_gain = query_gain.reshape(1, DH)
    key_gain = key_gain.reshape(1, DH)
    shape = jax.ShapeDtypeStruct

    rows = grad_output.shape[0]
    groups = NC * NL
    pieces = call(cut_kernel, shape((groups, rows, WIDE), BF16), 0, 1 << 18, (grad_output,))
    exchanged = lax.all_to_all(pieces, ("core", "zl"), 0, 0, tiled=True)
    gathered = lax.all_gather(exchanged, "y", axis=0)

    mixed, attention = call(
        forward_kernel,
        (shape((DH, TOK), BF16), shape((IMAGES, PATCH, PATCH), F32)),
        2 * 2 * IMAGES * PATCH * PATCH * DH,
        1 << 20,
        (query_input, key_input, value_input, query_gain, key_gain),
    )
    exchanged, out_weight = lax.optimization_barrier((exchanged, out_weight))
    moved = [cross(out_weight, shift) for shift in range(NZ)]
    mixed, *moved = lax.optimization_barrier((mixed, *moved))
    mixed_own = share(mixed, "zl", NL)
    own = lax.all_gather(jnp.stack(moved), "x", axis=0)
    mixed_own, own = lax.optimization_barrier((mixed_own, own))
    mixed_other = swap_cores(mixed_own)
    gathered, own, mixed_other = lax.optimization_barrier((gathered, own, mixed_other))

    half = (NL, TOK, DH)
    keep, send = call(
        heads_kernel,
        (shape(half, BF16), shape(half, BF16)),
        2 * TOK * NY * DH * WIDE,
        4 << 20,
        (gathered, own),
    )
    gathered, send = lax.optimization_barrier((gathered, send))
    received = swap_cores(send)
    partial = call(
        weight_kernel,
        shape((NL, NZ, DH, BLK), BF16),
        2 * TOK * NY * DH * WIDE,
        5 << 20,
        (gathered, mixed_own, mixed_other),
    )
    spread = lax.all_to_all(partial, "x", 0, 0, tiled=True)
    summed = (keep.astype(F32) + received.astype(F32)).astype(BF16)
    grad_heads = lax.psum_scatter(summed, "zl", scatter_dimension=0, tiled=True)
    by_zone = sum(spread[part].astype(F32) for part in range(NX)).astype(BF16)
    last = [cross(by_zone[shift], shift) for shift in range(NZ)]
    grad_weight = sum(entry.astype(F32) for entry in last).astype(BF16)

    grad_query, grad_key, grad_value = call(
        backward_kernel,
        (shape((TOK, DH), BF16),) * 3,
        5 * 2 * IMAGES * PATCH * PATCH * DH,
        2 << 20,
        (query_input, key_input, value_input, query_gain, key_gain, attention, grad_heads.reshape(TOK, DH)),
    )
    return grad_query, grad_key, grad_value, grad_weight


def solution(mesh):
    axes = ("zh", "x", "core", "y", "zl")
    fine = Mesh(mesh.devices.reshape(NZ, NX, NC, NY, NL), axes)
    tokens, heads = ("zh", "x", "core"), ("y", "zl")
    in_specs = (
        P(tokens, heads),
        P(tokens, heads),
        P(tokens, heads),
        P(),
        P(),
        P(heads, tokens),
        P(tokens + heads, None),
    )
    out_specs = (P(tokens, heads), P(tokens, heads), P(tokens, heads), P(heads, tokens))
    return jax.shard_map(shards, mesh=fine, in_specs=in_specs, out_specs=out_specs, check_vma=False)
```

```python
import functools
import math

import jax
import jax.numpy as jnp
from jax import lax
from jax.experimental import pallas as pl
from jax.experimental.pallas import tpu as pltpu
from jax.sharding import Mesh
from jax.sharding import PartitionSpec as P

DH = 128
PATCH = 256
IMAGES = 2
TOK = 512
NZ, NX, NC, NY, NL = 3, 4, 2, 8, 4
BLK = 256
WIDE = NZ * BLK
epsilon = 1e-06
F32 = jnp.float32
BF16 = jnp.bfloat16
VMEM_LIMIT = 12 * 1024 * 1024
SCALING = 1.0 / math.sqrt(DH)


def dot(a, b, ca, cb):
    return lax.dot_general(a, b, (((ca,), (cb,)), ((), ())), preferred_element_type=F32)


def normalize(inputs):
    inputs = inputs.astype(F32)
    average = jnp.mean(inputs, axis=-1, keepdims=True)
    centred = inputs - average
    inverse = lax.rsqrt(jnp.mean(centred * centred, axis=-1, keepdims=True) + epsilon)
    return centred * inverse, inverse


def norm_back(gradient, unit_rows, inverse, gain):
    scaled = gradient * gain
    return (
        scaled
        - jnp.mean(scaled, axis=-1, keepdims=True)
        - unit_rows * jnp.mean(scaled * unit_rows, axis=-1, keepdims=True)
    ) * inverse


def cut_kernel(go_ref, cut_ref):
    for zone in range(NZ):
        for low in range(NL):
            for core in range(NC):
                source = ((zone * NL + low) * NC + core) * BLK
                piece = go_ref[:, source : source + BLK]
                cut_ref[core * NL + low, :, zone * BLK : (zone + 1) * BLK] = piece


def forward_kernel(q_ref, k_ref, v_ref, qg_ref, kg_ref, mixed_ref, att_ref):
    for image in range(IMAGES):
        rows = pl.ds(image * PATCH, PATCH)
        query_low = (normalize(q_ref[rows, :])[0] * qg_ref[...]).astype(BF16)
        key_low = (normalize(k_ref[rows, :])[0] * kg_ref[...]).astype(BF16)
        exponent = jnp.exp(dot(query_low, key_low, 1, 1) * SCALING)
        attention = exponent / jnp.sum(exponent, axis=-1, keepdims=True)
        att_ref[image] = attention
        mixed = dot(v_ref[rows, :], attention.astype(BF16), 0, 1)
        mixed_ref[:, rows] = mixed.astype(BF16)


def backward_kernel(
    q_ref, k_ref, v_ref, qg_ref, kg_ref, att_ref, gh_ref, dq_ref, dk_ref, dv_ref
):
    for image in range(IMAGES):
        rows = pl.ds(image * PATCH, PATCH)
        grad_heads = gh_ref[rows, :]
        query_unit, query_inv = normalize(q_ref[rows, :])
        key_unit, key_inv = normalize(k_ref[rows, :])
        query_low = (query_unit * qg_ref[...]).astype(BF16)
        key_low = (key_unit * kg_ref[...]).astype(BF16)
        attention = att_ref[image]
        dv_ref[rows, :] = dot(attention.astype(BF16), grad_heads, 0, 0).astype(BF16)
        grad_attention = dot(grad_heads, v_ref[rows, :], 1, 1)
        row_delta = jnp.sum(attention * grad_attention, axis=-1, keepdims=True)
        grad_scores = (attention * (grad_attention - row_delta)).astype(BF16)
        grad_qn = dot(grad_scores, key_low, 1, 0) * SCALING
        grad_kn = dot(grad_scores, query_low, 0, 0) * SCALING
        dq_ref[rows, :] = norm_back(grad_qn, query_unit, query_inv, qg_ref[...]).astype(BF16)
        dk_ref[rows, :] = norm_back(grad_kn, key_unit, key_inv, kg_ref[...]).astype(BF16)


def block(ref, side, zone):
    columns = pl.ds(zone * BLK, BLK)
    return ref[:, pl.ds(side * NL, NL), :, columns].reshape(TOK, BLK)


def heads_kernel(g_ref, own_ref, keep_ref, send_ref):
    here, core = lax.axis_index("zh"), lax.axis_index("core")
    for ref, side in ((send_ref, 1 - core), (keep_ref, core)):
        total = None
        for step in range(NZ):
            rows = block(g_ref, side, lax.rem(here + NZ - step, NZ))
            term = dot(rows, own_ref[:, step].reshape(NL * DH, BLK), 1, 1)
            total = term if total is None else total + term
        for head in range(NL):
            ref[head] = total[:, head * DH : (head + 1) * DH].astype(BF16)


def weight_kernel(g_ref, own_ref, other_ref, keep_ref, received_ref, out_ref, summed_ref):
    for head in range(NL):
        both = keep_ref[head].astype(F32) + received_ref[head].astype(F32)
        summed_ref[head] = both.astype(BF16)
    here, core = lax.axis_index("zh"), lax.axis_index("core")
    own = own_ref[...].reshape(NL * DH, TOK)
    other = other_ref[...].reshape(NL * DH, TOK)
    for step in range(NZ):
        zone = lax.rem(here + step, NZ)
        total = dot(own, block(g_ref, core, zone), 1, 0)
        total = total + dot(other, block(g_ref, 1 - core, zone), 1, 0)
        out_ref[:, step] = total.reshape(NL, DH, BLK).astype(BF16)


def call(kernel, outs, flops, moved, operands):
    return pl.pallas_call(
        kernel,
        out_shape=outs,
        in_specs=[pl.BlockSpec(memory_space=pltpu.VMEM)] * len(operands),
        out_specs=jax.tree.map(lambda _: pl.BlockSpec(memory_space=pltpu.VMEM), outs),
        compiler_params=pltpu.CompilerParams(vmem_limit_bytes=VMEM_LIMIT),
        cost_estimate=pl.CostEstimate(flops=flops, bytes_accessed=moved, transcendentals=0),
    )(*operands)


def cross(entry, shift):
    pairs = []
    for zone in range(NZ):
        for across in range(NX):
            for low in range(NL):
                target = (zone + shift) % NZ
                pairs.append(
                    ((zone * NX + across) * NL + low, (target * NX + low) * NL + across)
                )
    return lax.ppermute(entry, ("zh", "x", "zl"), pairs)


def share(entry, axis, size):
    copies = jnp.broadcast_to(entry[None], (size,) + entry.shape)
    return lax.all_to_all(copies, axis, 0, 0, tiled=True)


def swap_cores(entry):
    return lax.ppermute(entry, "core", [(0, 1), (1, 0)])


def shards(query_input, key_input, value_input, query_gain, key_gain, out_weight, grad_output):
    query_gain = query_gain.reshape(1, DH)
    key_gain = key_gain.reshape(1, DH)
    shape = jax.ShapeDtypeStruct

    rows = grad_output.shape[0]
    groups = NC * NL
    pieces = call(cut_kernel, shape((groups, rows, WIDE), BF16), 0, 1 << 18, (grad_output,))
    exchanged = lax.all_to_all(pieces, ("core", "zl"), 0, 0, tiled=True)
    mixed, attention = call(
        forward_kernel,
        (shape((DH, TOK), BF16), shape((IMAGES, PATCH, PATCH), F32)),
        2 * 2 * IMAGES * PATCH * PATCH * DH,
        1 << 20,
        (query_input, key_input, value_input, query_gain, key_gain),
    )
    exchanged, out_weight, mixed = lax.optimization_barrier((exchanged, out_weight, mixed))
    gathered = lax.all_gather(exchanged, "y", axis=0)
    moved = [cross(out_weight, shift) for shift in range(NZ)]
    mixed, *moved = lax.optimization_barrier((mixed, *moved))
    mixed_own = share(mixed, "zl", NL)
    own = lax.all_gather(jnp.stack(moved), "x", axis=0)
    mixed_own, own = lax.optimization_barrier((mixed_own, own))
    mixed_other = swap_cores(mixed_own)
    gathered, own, mixed_other = lax.optimization_barrier((gathered, own, mixed_other))

    half = (NL, TOK, DH)
    keep, send = call(
        heads_kernel,
        (shape(half, BF16), shape(half, BF16)),
        2 * TOK * NY * DH * WIDE,
        4 << 20,
        (gathered, own),
    )
    received = swap_cores(send)
    partial, summed = call(
        weight_kernel,
        (shape((NL, NZ, DH, BLK), BF16), shape(half, BF16)),
        2 * TOK * NY * DH * WIDE,
        5 << 20,
        (gathered, mixed_own, mixed_other, keep, received),
    )
    spread = lax.all_to_all(partial, "x", 0, 0, tiled=True)
    grad_heads = lax.psum_scatter(summed, "zl", scatter_dimension=0, tiled=True)
    by_zone = sum(spread[part].astype(F32) for part in range(NX)).astype(BF16)
    last = [cross(by_zone[shift], shift) for shift in range(NZ)]
    grad_query, grad_key, grad_value = call(
        backward_kernel,
        (shape((TOK, DH), BF16),) * 3,
        5 * 2 * IMAGES * PATCH * PATCH * DH,
        2 << 20,
        (query_input, key_input, value_input, query_gain, key_gain, attention, grad_heads.reshape(TOK, DH)),
    )
    grad_query, grad_key, grad_value, *last = lax.optimization_barrier(
        (grad_query, grad_key, grad_value, *last)
    )
    grad_weight = sum(entry.astype(F32) for entry in last).astype(BF16)
    return grad_query, grad_key, grad_value, grad_weight


def solution(mesh):
    axes = ("zh", "x", "core", "y", "zl")
    fine = Mesh(mesh.devices.reshape(NZ, NX, NC, NY, NL), axes)
    tokens, heads = ("zh", "x", "core"), ("y", "zl")
    in_specs = (
        P(tokens, heads),
        P(tokens, heads),
        P(tokens, heads),
        P(),
        P(),
        P(heads, tokens),
        P(tokens + heads, None),
    )
    out_specs = (P(tokens, heads), P(tokens, heads), P(tokens, heads), P(heads, tokens))
    return jax.shard_map(shards, mesh=fine, in_specs=in_specs, out_specs=out_specs, check_vma=False)
```

```python
import functools
import math

import jax
import jax.numpy as jnp
from jax import lax
from jax.experimental import pallas as pl
from jax.experimental.pallas import tpu as pltpu
from jax.sharding import Mesh
from jax.sharding import PartitionSpec as P

DH = 128
PATCH = 256
IMAGES = 2
TOK = 512
NZ, NX, NC, NY, NL = 3, 4, 2, 8, 4
BLK = 256
WIDE = NZ * BLK
epsilon = 1e-06
F32 = jnp.float32
BF16 = jnp.bfloat16
VMEM_LIMIT = 12 * 1024 * 1024
SCALING = 1.0 / math.sqrt(DH)


def dot(a, b, ca, cb):
    return lax.dot_general(a, b, (((ca,), (cb,)), ((), ())), preferred_element_type=F32)


def normalize(inputs):
    inputs = inputs.astype(F32)
    average = jnp.mean(inputs, axis=-1, keepdims=True)
    centred = inputs - average
    inverse = lax.rsqrt(jnp.mean(centred * centred, axis=-1, keepdims=True) + epsilon)
    return centred * inverse, inverse


def norm_back(gradient, unit_rows, inverse, gain):
    scaled = gradient * gain
    return (
        scaled
        - jnp.mean(scaled, axis=-1, keepdims=True)
        - unit_rows * jnp.mean(scaled * unit_rows, axis=-1, keepdims=True)
    ) * inverse


def cut_kernel(go_ref, cut_ref):
    for zone in range(NZ):
        for low in range(NL):
            for core in range(NC):
                source = ((zone * NL + low) * NC + core) * BLK
                piece = go_ref[:, source : source + BLK]
                cut_ref[core * NL + low, :, zone * BLK : (zone + 1) * BLK] = piece


def forward_kernel(q_ref, k_ref, v_ref, qg_ref, kg_ref, mixed_ref, att_ref):
    for image in range(IMAGES):
        rows = pl.ds(image * PATCH, PATCH)
        query_low = (normalize(q_ref[rows, :])[0] * qg_ref[...]).astype(BF16)
        key_low = (normalize(k_ref[rows, :])[0] * kg_ref[...]).astype(BF16)
        exponent = jnp.exp(dot(query_low, key_low, 1, 1) * SCALING)
        attention = exponent / jnp.sum(exponent, axis=-1, keepdims=True)
        att_ref[image] = attention
        mixed = dot(v_ref[rows, :], attention.astype(BF16), 0, 1)
        mixed_ref[:, rows] = mixed.astype(BF16)


def backward_kernel(
    q_ref, k_ref, v_ref, qg_ref, kg_ref, att_ref, gh_ref, dq_ref, dk_ref, dv_ref
):
    for image in range(IMAGES):
        rows = pl.ds(image * PATCH, PATCH)
        grad_heads = gh_ref[rows, :]
        query_unit, query_inv = normalize(q_ref[rows, :])
        key_unit, key_inv = normalize(k_ref[rows, :])
        query_low = (query_unit * qg_ref[...]).astype(BF16)
        key_low = (key_unit * kg_ref[...]).astype(BF16)
        attention = att_ref[image]
        dv_ref[rows, :] = dot(attention.astype(BF16), grad_heads, 0, 0).astype(BF16)
        grad_attention = dot(grad_heads, v_ref[rows, :], 1, 1)
        row_delta = jnp.sum(attention * grad_attention, axis=-1, keepdims=True)
        grad_scores = (attention * (grad_attention - row_delta)).astype(BF16)
        grad_qn = dot(grad_scores, key_low, 1, 0) * SCALING
        grad_kn = dot(grad_scores, query_low, 0, 0) * SCALING
        dq_ref[rows, :] = norm_back(grad_qn, query_unit, query_inv, qg_ref[...]).astype(BF16)
        dk_ref[rows, :] = norm_back(grad_kn, key_unit, key_inv, kg_ref[...]).astype(BF16)


def block(ref, side, zone):
    columns = slice(zone * BLK, (zone + 1) * BLK)
    return ref[:, pl.ds(side * NL, NL), :, columns].reshape(TOK, BLK)


def heads_kernel(g_ref, own_ref, keep_ref, send_ref):
    core = lax.axis_index("core")
    for ref, side in ((send_ref, 1 - core), (keep_ref, core)):
        total = None
        for step in range(NZ):
            rows = block(g_ref, side, step)
            term = dot(rows, own_ref[:, step].reshape(NL * DH, BLK), 1, 1)
            total = term if total is None else total + term
        for head in range(NL):
            ref[head] = total[:, head * DH : (head + 1) * DH].astype(BF16)


def weight_kernel(g_ref, own_ref, other_ref, out_ref):
    core = lax.axis_index("core")
    own = own_ref[...].reshape(NL * DH, TOK)
    other = other_ref[...].reshape(NL * DH, TOK)
    for step in range(NZ):
        total = dot(own, block(g_ref, core, step), 1, 0)
        total = total + dot(other, block(g_ref, 1 - core, step), 1, 0)
        out_ref[:, step] = total.reshape(NL, DH, BLK).astype(BF16)


def call(kernel, outs, flops, moved, operands):
    return pl.pallas_call(
        kernel,
        out_shape=outs,
        in_specs=[pl.BlockSpec(memory_space=pltpu.VMEM)] * len(operands),
        out_specs=jax.tree.map(lambda _: pl.BlockSpec(memory_space=pltpu.VMEM), outs),
        compiler_params=pltpu.CompilerParams(vmem_limit_bytes=VMEM_LIMIT),
        cost_estimate=pl.CostEstimate(flops=flops, bytes_accessed=moved, transcendentals=0),
    )(*operands)


def cross(entry):
    pairs = [(at * NL + low, low * NL + at) for at in range(NX) for low in range(NL)]
    return lax.ppermute(entry, ("x", "zl"), pairs)


def share(entry, axis, size):
    copies = jnp.broadcast_to(entry[None], (size,) + entry.shape)
    return lax.all_to_all(copies, axis, 0, 0, tiled=True)


def swap_cores(entry):
    return lax.ppermute(entry, "core", [(0, 1), (1, 0)])


def shards(query_input, key_input, value_input, query_gain, key_gain, out_weight, grad_output):
    query_gain = query_gain.reshape(1, DH)
    key_gain = key_gain.reshape(1, DH)
    shape = jax.ShapeDtypeStruct

    rows = grad_output.shape[0]
    groups = NC * NL
    pieces = call(cut_kernel, shape((groups, rows, WIDE), BF16), 0, 1 << 18, (grad_output,))
    exchanged = lax.all_to_all(pieces, ("core", "zl"), 0, 0, tiled=True)
    gathered = lax.all_gather(exchanged, "y", axis=0)

    mixed, attention = call(
        forward_kernel,
        (shape((DH, TOK), BF16), shape((IMAGES, PATCH, PATCH), F32)),
        2 * 2 * IMAGES * PATCH * PATCH * DH,
        1 << 20,
        (query_input, key_input, value_input, query_gain, key_gain),
    )
    exchanged, out_weight = lax.optimization_barrier((exchanged, out_weight))
    zones = share(cross(out_weight), "zh", NZ)
    mixed, zones = lax.optimization_barrier((mixed, zones))
    mixed_own = share(mixed, "zl", NL)
    own = lax.all_gather(zones, "x", axis=0)
    mixed_own, own = lax.optimization_barrier((mixed_own, own))
    mixed_other = swap_cores(mixed_own)
    gathered, own, mixed_other = lax.optimization_barrier((gathered, own, mixed_other))

    half = (NL, TOK, DH)
    keep, send = call(
        heads_kernel,
        (shape(half, BF16), shape(half, BF16)),
        2 * TOK * NY * DH * WIDE,
        4 << 20,
        (gathered, own),
    )
    gathered, send = lax.optimization_barrier((gathered, send))
    received = swap_cores(send)
    partial = call(
        weight_kernel,
        shape((NL, NZ, DH, BLK), BF16),
        2 * TOK * NY * DH * WIDE,
        5 << 20,
        (gathered, mixed_own, mixed_other),
    )
    spread = lax.all_to_all(partial, "x", 0, 0, tiled=True)
    summed = (keep.astype(F32) + received.astype(F32)).astype(BF16)
    grad_heads = lax.psum_scatter(summed, "zl", scatter_dimension=0, tiled=True)
    by_zone = sum(spread[part].astype(F32) for part in range(NX)).astype(BF16)
    last = lax.all_to_all(by_zone, "zh", 0, 0, tiled=True)
    grad_weight = cross(sum(last[zone].astype(F32) for zone in range(NZ)).astype(BF16))

    grad_query, grad_key, grad_value = call(
        backward_kernel,
        (shape((TOK, DH), BF16),) * 3,
        5 * 2 * IMAGES * PATCH * PATCH * DH,
        2 << 20,
        (query_input, key_input, value_input, query_gain, key_gain, attention, grad_heads.reshape(TOK, DH)),
    )
    return grad_query, grad_key, grad_value, grad_weight


def solution(mesh):
    axes = ("zh", "x", "core", "y", "zl")
    fine = Mesh(mesh.devices.reshape(NZ, NX, NC, NY, NL), axes)
    tokens, heads = ("zh", "x", "core"), ("y", "zl")
    in_specs = (
        P(tokens, heads),
        P(tokens, heads),
        P(tokens, heads),
        P(),
        P(),
        P(heads, tokens),
        P(tokens + heads, None),
    )
    out_specs = (P(tokens, heads), P(tokens, heads), P(tokens, heads), P(heads, tokens))
    return jax.shard_map(shards, mesh=fine, in_specs=in_specs, out_specs=out_specs, check_vma=False)
```

```python
import functools
import math

import jax
import jax.numpy as jnp
from jax import lax
from jax.experimental import pallas as pl
from jax.experimental.pallas import tpu as pltpu
from jax.sharding import Mesh
from jax.sharding import PartitionSpec as P

DH = 128
PATCH = 256
IMAGES = 2
TOK = 512
NZ, NX, NC, NY, NL = 3, 4, 2, 8, 4
BLK = 256
WIDE = NZ * BLK
epsilon = 1e-06
F32 = jnp.float32
BF16 = jnp.bfloat16
VMEM_LIMIT = 12 * 1024 * 1024
SCALING = 1.0 / math.sqrt(DH)


def dot(a, b, ca, cb):
    return lax.dot_general(a, b, (((ca,), (cb,)), ((), ())), preferred_element_type=F32)


def normalize(inputs):
    inputs = inputs.astype(F32)
    average = jnp.mean(inputs, axis=-1, keepdims=True)
    centred = inputs - average
    inverse = lax.rsqrt(jnp.mean(centred * centred, axis=-1, keepdims=True) + epsilon)
    return centred * inverse, inverse


def norm_back(gradient, unit_rows, inverse, gain):
    scaled = gradient * gain
    return (
        scaled
        - jnp.mean(scaled, axis=-1, keepdims=True)
        - unit_rows * jnp.mean(scaled * unit_rows, axis=-1, keepdims=True)
    ) * inverse


def cut_kernel(go_ref, cut_ref):
    for zone in range(NZ):
        for low in range(NL):
            for core in range(NC):
                source = ((zone * NL + low) * NC + core) * BLK
                piece = go_ref[:, source : source + BLK]
                cut_ref[core * NL + low, :, zone * BLK : (zone + 1) * BLK] = piece


def forward_kernel(q_ref, k_ref, v_ref, qg_ref, kg_ref, mixed_ref, att_ref):
    for image in range(IMAGES):
        rows = pl.ds(image * PATCH, PATCH)
        query_low = (normalize(q_ref[rows, :])[0] * qg_ref[...]).astype(BF16)
        key_low = (normalize(k_ref[rows, :])[0] * kg_ref[...]).astype(BF16)
        exponent = jnp.exp(dot(query_low, key_low, 1, 1) * SCALING)
        attention = exponent / jnp.sum(exponent, axis=-1, keepdims=True)
        att_ref[image] = attention
        mixed = dot(v_ref[rows, :], attention.astype(BF16), 0, 1)
        mixed_ref[:, rows] = mixed.astype(BF16)


def backward_kernel(
    q_ref, k_ref, v_ref, qg_ref, kg_ref, att_ref, gh_ref, dq_ref, dk_ref, dv_ref
):
    for image in range(IMAGES):
        rows = pl.ds(image * PATCH, PATCH)
        grad_heads = gh_ref[rows, :]
        query_unit, query_inv = normalize(q_ref[rows, :])
        key_unit, key_inv = normalize(k_ref[rows, :])
        query_low = (query_unit * qg_ref[...]).astype(BF16)
        key_low = (key_unit * kg_ref[...]).astype(BF16)
        attention = att_ref[image]
        dv_ref[rows, :] = dot(attention.astype(BF16), grad_heads, 0, 0).astype(BF16)
        grad_attention = dot(grad_heads, v_ref[rows, :], 1, 1)
        row_delta = jnp.sum(attention * grad_attention, axis=-1, keepdims=True)
        grad_scores = (attention * (grad_attention - row_delta)).astype(BF16)
        grad_qn = dot(grad_scores, key_low, 1, 0) * SCALING
        grad_kn = dot(grad_scores, query_low, 0, 0) * SCALING
        dq_ref[rows, :] = norm_back(grad_qn, query_unit, query_inv, qg_ref[...]).astype(BF16)
        dk_ref[rows, :] = norm_back(grad_kn, key_unit, key_inv, kg_ref[...]).astype(BF16)


def block(ref, side, zone):
    columns = slice(zone * BLK, (zone + 1) * BLK)
    return ref[:, pl.ds(side * NL, NL), :, columns].reshape(TOK, BLK)


def heads_kernel(g_ref, own_ref, keep_ref, send_ref):
    core = lax.axis_index("core")
    for ref, side in ((send_ref, 1 - core), (keep_ref, core)):
        total = None
        for step in range(NZ):
            rows = block(g_ref, side, step)
            term = dot(rows, own_ref[:, step].reshape(NL * DH, BLK), 1, 1)
            total = term if total is None else total + term
        for head in range(NL):
            ref[head] = total[:, head * DH : (head + 1) * DH].astype(BF16)


def weight_kernel(g_ref, own_ref, other_ref, out_ref):
    core = lax.axis_index("core")
    own = own_ref[...].reshape(NL * DH, TOK)
    other = other_ref[...].reshape(NL * DH, TOK)
    for step in range(NZ):
        total = dot(own, block(g_ref, core, step), 1, 0)
        total = total + dot(other, block(g_ref, 1 - core, step), 1, 0)
        out_ref[:, step] = total.reshape(NL, DH, BLK).astype(BF16)


def call(kernel, outs, flops, moved, operands):
    return pl.pallas_call(
        kernel,
        out_shape=outs,
        in_specs=[pl.BlockSpec(memory_space=pltpu.VMEM)] * len(operands),
        out_specs=jax.tree.map(lambda _: pl.BlockSpec(memory_space=pltpu.VMEM), outs),
        compiler_params=pltpu.CompilerParams(vmem_limit_bytes=VMEM_LIMIT),
        cost_estimate=pl.CostEstimate(flops=flops, bytes_accessed=moved, transcendentals=0),
    )(*operands)


def cross(entry):
    pairs = [(at * NL + low, low * NL + at) for at in range(NX) for low in range(NL)]
    return lax.ppermute(entry, ("x", "zl"), pairs)


def share(entry, axis, size):
    copies = jnp.broadcast_to(entry[None], (size,) + entry.shape)
    return lax.all_to_all(copies, axis, 0, 0, tiled=True)


def swap_cores(entry):
    return lax.ppermute(entry, "core", [(0, 1), (1, 0)])


def shards(query_input, key_input, value_input, query_gain, key_gain, out_weight, grad_output):
    query_gain = query_gain.reshape(1, DH)
    key_gain = key_gain.reshape(1, DH)
    shape = jax.ShapeDtypeStruct

    rows = grad_output.shape[0]
    groups = NC * NL
    pieces = call(cut_kernel, shape((groups, rows, WIDE), BF16), 0, 1 << 18, (grad_output,))
    exchanged = lax.all_to_all(pieces, ("core", "zl"), 0, 0, tiled=True)
    gathered = lax.all_gather(exchanged, "y", axis=0)

    mixed, attention = call(
        forward_kernel,
        (shape((DH, TOK), BF16), shape((IMAGES, PATCH, PATCH), F32)),
        2 * 2 * IMAGES * PATCH * PATCH * DH,
        1 << 20,
        (query_input, key_input, value_input, query_gain, key_gain),
    )
    exchanged, out_weight = lax.optimization_barrier((exchanged, out_weight))
    crossed = cross(out_weight)
    mixed, crossed = lax.optimization_barrier((mixed, crossed))
    mixed_own = share(mixed, "zl", NL)
    zones = lax.all_gather(crossed, "zh", axis=0)
    mixed_own, zones = lax.optimization_barrier((mixed_own, zones))
    mixed_other = swap_cores(mixed_own)
    own = lax.all_gather(zones, "x", axis=0)
    gathered, own, mixed_other = lax.optimization_barrier((gathered, own, mixed_other))

    half = (NL, TOK, DH)
    keep, send = call(
        heads_kernel,
        (shape(half, BF16), shape(half, BF16)),
        2 * TOK * NY * DH * WIDE,
        4 << 20,
        (gathered, own),
    )
    gathered, send = lax.optimization_barrier((gathered, send))
    received = swap_cores(send)
    partial = call(
        weight_kernel,
        shape((NL, NZ, DH, BLK), BF16),
        2 * TOK * NY * DH * WIDE,
        5 << 20,
        (gathered, mixed_own, mixed_other),
    )
    spread = lax.all_to_all(partial, "x", 0, 0, tiled=True)
    summed = (keep.astype(F32) + received.astype(F32)).astype(BF16)
    grad_heads = lax.psum_scatter(summed, "zl", scatter_dimension=0, tiled=True)
    by_zone = sum(spread[part].astype(F32) for part in range(NX)).astype(BF16)
    last = lax.all_to_all(by_zone, "zh", 0, 0, tiled=True)
    grad_weight = cross(sum(last[zone].astype(F32) for zone in range(NZ)).astype(BF16))

    grad_query, grad_key, grad_value = call(
        backward_kernel,
        (shape((TOK, DH), BF16),) * 3,
        5 * 2 * IMAGES * PATCH * PATCH * DH,
        2 << 20,
        (query_input, key_input, value_input, query_gain, key_gain, attention, grad_heads.reshape(TOK, DH)),
    )
    return grad_query, grad_key, grad_value, grad_weight


def solution(mesh):
    axes = ("zh", "x", "core", "y", "zl")
    fine = Mesh(mesh.devices.reshape(NZ, NX, NC, NY, NL), axes)
    tokens, heads = ("zh", "x", "core"), ("y", "zl")
    in_specs = (
        P(tokens, heads),
        P(tokens, heads),
        P(tokens, heads),
        P(),
        P(),
        P(heads, tokens),
        P(tokens + heads, None),
    )
    out_specs = (P(tokens, heads), P(tokens, heads), P(tokens, heads), P(heads, tokens))
    return jax.shard_map(shards, mesh=fine, in_specs=in_specs, out_specs=out_specs, check_vma=False)
```

```python
import functools
import math

import jax
import jax.numpy as jnp
from jax import lax
from jax.experimental import pallas as pl
from jax.experimental.pallas import tpu as pltpu
from jax.sharding import Mesh
from jax.sharding import PartitionSpec as P

DH = 128
PATCH = 256
IMAGES = 2
TOK = 512
NZ, NX, NC, NY, NL = 3, 4, 2, 8, 4
BLK = 256
WIDE = NZ * BLK
epsilon = 1e-06
F32 = jnp.float32
BF16 = jnp.bfloat16
VMEM_LIMIT = 12 * 1024 * 1024
SCALING = 1.0 / math.sqrt(DH)


def dot(a, b, ca, cb):
    return lax.dot_general(a, b, (((ca,), (cb,)), ((), ())), preferred_element_type=F32)


def normalize(inputs):
    inputs = inputs.astype(F32)
    average = jnp.mean(inputs, axis=-1, keepdims=True)
    centred = inputs - average
    inverse = lax.rsqrt(jnp.mean(centred * centred, axis=-1, keepdims=True) + epsilon)
    return centred * inverse, inverse


def norm_back(gradient, unit_rows, inverse, gain):
    scaled = gradient * gain
    return (
        scaled
        - jnp.mean(scaled, axis=-1, keepdims=True)
        - unit_rows * jnp.mean(scaled * unit_rows, axis=-1, keepdims=True)
    ) * inverse


def cut_kernel(go_ref, cut_ref):
    for zone in range(NZ):
        for low in range(NL):
            for core in range(NC):
                source = ((zone * NL + low) * NC + core) * BLK
                piece = go_ref[:, source : source + BLK]
                cut_ref[core * NL + low, :, zone * BLK : (zone + 1) * BLK] = piece


def forward_kernel(q_ref, k_ref, v_ref, qg_ref, kg_ref, mixed_ref, att_ref):
    for image in range(IMAGES):
        rows = pl.ds(image * PATCH, PATCH)
        query_low = (normalize(q_ref[rows, :])[0] * qg_ref[...]).astype(BF16)
        key_low = (normalize(k_ref[rows, :])[0] * kg_ref[...]).astype(BF16)
        exponent = jnp.exp(dot(query_low, key_low, 1, 1) * SCALING)
        attention = exponent / jnp.sum(exponent, axis=-1, keepdims=True)
        att_ref[image] = attention
        mixed = dot(v_ref[rows, :], attention.astype(BF16), 0, 1)
        mixed_ref[:, rows] = mixed.astype(BF16)


def backward_kernel(
    q_ref, k_ref, v_ref, qg_ref, kg_ref, att_ref, gh_ref, dq_ref, dk_ref, dv_ref
):
    for image in range(IMAGES):
        rows = pl.ds(image * PATCH, PATCH)
        grad_heads = gh_ref[rows, :]
        query_unit, query_inv = normalize(q_ref[rows, :])
        key_unit, key_inv = normalize(k_ref[rows, :])
        query_low = (query_unit * qg_ref[...]).astype(BF16)
        key_low = (key_unit * kg_ref[...]).astype(BF16)
        attention = att_ref[image]
        dv_ref[rows, :] = dot(attention.astype(BF16), grad_heads, 0, 0).astype(BF16)
        grad_attention = dot(grad_heads, v_ref[rows, :], 1, 1)
        row_delta = jnp.sum(attention * grad_attention, axis=-1, keepdims=True)
        grad_scores = (attention * (grad_attention - row_delta)).astype(BF16)
        grad_qn = dot(grad_scores, key_low, 1, 0) * SCALING
        grad_kn = dot(grad_scores, query_low, 0, 0) * SCALING
        dq_ref[rows, :] = norm_back(grad_qn, query_unit, query_inv, qg_ref[...]).astype(BF16)
        dk_ref[rows, :] = norm_back(grad_kn, key_unit, key_inv, kg_ref[...]).astype(BF16)


def block(ref, side, zone):
    columns = slice(zone * BLK, (zone + 1) * BLK)
    return ref[:, pl.ds(side * NL, NL), :, columns].reshape(TOK, BLK)


def heads_kernel(g_ref, own_ref, keep_ref, send_ref):
    core = lax.axis_index("core")
    for ref, side in ((send_ref, 1 - core), (keep_ref, core)):
        total = None
        for step in range(NZ):
            rows = block(g_ref, side, step)
            term = dot(rows, own_ref[:, step].reshape(NL * DH, BLK), 1, 1)
            total = term if total is None else total + term
        for head in range(NL):
            ref[head] = total[:, head * DH : (head + 1) * DH].astype(BF16)


def weight_kernel(g_ref, own_ref, other_ref, out_ref):
    core = lax.axis_index("core")
    own = own_ref[...].reshape(NL * DH, TOK)
    other = other_ref[...].reshape(NL * DH, TOK)
    for step in range(NZ):
        total = dot(own, block(g_ref, core, step), 1, 0)
        total = total + dot(other, block(g_ref, 1 - core, step), 1, 0)
        out_ref[:, step] = total.reshape(NL, DH, BLK).astype(BF16)


def call(kernel, outs, flops, moved, operands):
    return pl.pallas_call(
        kernel,
        out_shape=outs,
        in_specs=[pl.BlockSpec(memory_space=pltpu.VMEM)] * len(operands),
        out_specs=jax.tree.map(lambda _: pl.BlockSpec(memory_space=pltpu.VMEM), outs),
        compiler_params=pltpu.CompilerParams(vmem_limit_bytes=VMEM_LIMIT),
        cost_estimate=pl.CostEstimate(flops=flops, bytes_accessed=moved, transcendentals=0),
    )(*operands)


def cross(entry):
    pairs = [(at * NL + low, low * NL + at) for at in range(NX) for low in range(NL)]
    return lax.ppermute(entry, ("x", "zl"), pairs)


def share(entry, axis, size):
    copies = jnp.broadcast_to(entry[None], (size,) + entry.shape)
    return lax.all_to_all(copies, axis, 0, 0, tiled=True)


def swap_cores(entry):
    return lax.ppermute(entry, "core", [(0, 1), (1, 0)])


def shards(query_input, key_input, value_input, query_gain, key_gain, out_weight, grad_output):
    query_gain = query_gain.reshape(1, DH)
    key_gain = key_gain.reshape(1, DH)
    shape = jax.ShapeDtypeStruct

    rows = grad_output.shape[0]
    groups = NC * NL
    pieces = call(cut_kernel, shape((groups, rows, WIDE), BF16), 0, 1 << 18, (grad_output,))
    exchanged = lax.all_to_all(pieces, ("core", "zl"), 0, 0, tiled=True)

    mixed, attention = call(
        forward_kernel,
        (shape((DH, TOK), BF16), shape((IMAGES, PATCH, PATCH), F32)),
        2 * 2 * IMAGES * PATCH * PATCH * DH,
        1 << 20,
        (query_input, key_input, value_input, query_gain, key_gain),
    )
    exchanged, crossed = lax.optimization_barrier((exchanged, cross(out_weight)))
    gathered = lax.all_gather(exchanged, "y", axis=0)
    zones = share(crossed, "zh", NZ)
    mixed, zones = lax.optimization_barrier((mixed, zones))
    mixed_own = share(mixed, "zl", NL)
    own = lax.all_gather(zones, "x", axis=0)
    mixed_own, own = lax.optimization_barrier((mixed_own, own))
    mixed_other = swap_cores(mixed_own)
    gathered, own, mixed_other = lax.optimization_barrier((gathered, own, mixed_other))

    half = (NL, TOK, DH)
    keep, send = call(
        heads_kernel,
        (shape(half, BF16), shape(half, BF16)),
        2 * TOK * NY * DH * WIDE,
        4 << 20,
        (gathered, own),
    )
    gathered, send = lax.optimization_barrier((gathered, send))
    received = swap_cores(send)
    partial = call(
        weight_kernel,
        shape((NL, NZ, DH, BLK), BF16),
        2 * TOK * NY * DH * WIDE,
        5 << 20,
        (gathered, mixed_own, mixed_other),
    )
    spread = lax.all_to_all(partial, "x", 0, 0, tiled=True)
    summed = (keep.astype(F32) + received.astype(F32)).astype(BF16)
    grad_heads = lax.psum_scatter(summed, "zl", scatter_dimension=0, tiled=True)
    by_zone = sum(spread[part].astype(F32) for part in range(NX)).astype(BF16)
    last = lax.all_to_all(by_zone, "zh", 0, 0, tiled=True)
    grad_weight = cross(sum(last[zone].astype(F32) for zone in range(NZ)).astype(BF16))

    grad_query, grad_key, grad_value = call(
        backward_kernel,
        (shape((TOK, DH), BF16),) * 3,
        5 * 2 * IMAGES * PATCH * PATCH * DH,
        2 << 20,
        (query_input, key_input, value_input, query_gain, key_gain, attention, grad_heads.reshape(TOK, DH)),
    )
    return grad_query, grad_key, grad_value, grad_weight


def solution(mesh):
    axes = ("zh", "x", "core", "y", "zl")
    fine = Mesh(mesh.devices.reshape(NZ, NX, NC, NY, NL), axes)
    tokens, heads = ("zh", "x", "core"), ("y", "zl")
    in_specs = (
        P(tokens, heads),
        P(tokens, heads),
        P(tokens, heads),
        P(),
        P(),
        P(heads, tokens),
        P(tokens + heads, None),
    )
    out_specs = (P(tokens, heads), P(tokens, heads), P(tokens, heads), P(heads, tokens))
    return jax.shard_map(shards, mesh=fine, in_specs=in_specs, out_specs=out_specs, check_vma=False)
```

```python
import functools
import math

import jax
import jax.numpy as jnp
from jax import lax
from jax.experimental import pallas as pl
from jax.experimental.pallas import tpu as pltpu
from jax.sharding import Mesh
from jax.sharding import PartitionSpec as P

DH = 128
PATCH = 256
IMAGES = 2
TOK = 512
NZ, NX, NC, NY, NL = 3, 4, 2, 8, 4
BLK = 256
WIDE = NZ * BLK
epsilon = 1e-06
F32 = jnp.float32
BF16 = jnp.bfloat16
VMEM_LIMIT = 12 * 1024 * 1024
SCALING = 1.0 / math.sqrt(DH)


def dot(a, b, ca, cb):
    return lax.dot_general(a, b, (((ca,), (cb,)), ((), ())), preferred_element_type=F32)


def normalize(inputs):
    inputs = inputs.astype(F32)
    average = jnp.mean(inputs, axis=-1, keepdims=True)
    centred = inputs - average
    inverse = lax.rsqrt(jnp.mean(centred * centred, axis=-1, keepdims=True) + epsilon)
    return centred * inverse, inverse


def norm_back(gradient, unit_rows, inverse, gain):
    scaled = gradient * gain
    return (
        scaled
        - jnp.mean(scaled, axis=-1, keepdims=True)
        - unit_rows * jnp.mean(scaled * unit_rows, axis=-1, keepdims=True)
    ) * inverse


def cut_kernel(go_ref, cut_ref):
    for zone in range(NZ):
        for low in range(NL):
            for core in range(NC):
                source = ((zone * NL + low) * NC + core) * BLK
                piece = go_ref[:, source : source + BLK]
                cut_ref[core * NL + low, :, zone * BLK : (zone + 1) * BLK] = piece


def forward_kernel(q_ref, k_ref, v_ref, qg_ref, kg_ref, mixed_ref, att_ref):
    for image in range(IMAGES):
        rows = pl.ds(image * PATCH, PATCH)
        query_low = (normalize(q_ref[rows, :])[0] * qg_ref[...]).astype(BF16)
        key_low = (normalize(k_ref[rows, :])[0] * kg_ref[...]).astype(BF16)
        exponent = jnp.exp(dot(query_low, key_low, 1, 1) * SCALING)
        attention = exponent / jnp.sum(exponent, axis=-1, keepdims=True)
        att_ref[image] = attention
        mixed = dot(v_ref[rows, :], attention.astype(BF16), 0, 1)
        mixed_ref[:, rows] = mixed.astype(BF16)


def backward_kernel(q_ref, k_ref, v_ref, qg_ref, kg_ref, att_ref, *refs):
    gh_refs, (dq_ref, dk_ref, dv_ref) = refs[:NL], refs[NL:]
    for image in range(IMAGES):
        rows = pl.ds(image * PATCH, PATCH)
        total = gh_refs[0][rows, :].astype(F32)
        for part in range(1, NL):
            total = total + gh_refs[part][rows, :].astype(F32)
        grad_heads = total.astype(BF16)
        query_unit, query_inv = normalize(q_ref[rows, :])
        key_unit, key_inv = normalize(k_ref[rows, :])
        query_low = (query_unit * qg_ref[...]).astype(BF16)
        key_low = (key_unit * kg_ref[...]).astype(BF16)
        attention = att_ref[image]
        dv_ref[rows, :] = dot(attention.astype(BF16), grad_heads, 0, 0).astype(BF16)
        grad_attention = dot(grad_heads, v_ref[rows, :], 1, 1)
        row_delta = jnp.sum(attention * grad_attention, axis=-1, keepdims=True)
        grad_scores = (attention * (grad_attention - row_delta)).astype(BF16)
        grad_qn = dot(grad_scores, key_low, 1, 0) * SCALING
        grad_kn = dot(grad_scores, query_low, 0, 0) * SCALING
        dq_ref[rows, :] = norm_back(grad_qn, query_unit, query_inv, qg_ref[...]).astype(BF16)
        dk_ref[rows, :] = norm_back(grad_kn, key_unit, key_inv, kg_ref[...]).astype(BF16)


def block(ref, side, zone):
    columns = slice(zone * BLK, (zone + 1) * BLK)
    return ref[:, pl.ds(side * NL, NL), :, columns].reshape(TOK, BLK)


def heads_kernel(g_ref, own_ref, keep_ref, send_ref):
    core, low = lax.axis_index("core"), lax.axis_index("zl")
    for ref, side in ((send_ref, 1 - core), (keep_ref, core)):
        total = None
        for zone in range(NZ):
            weight = jnp.concatenate([own_ref[low ^ step, zone] for step in range(NL)], axis=0)
            term = dot(block(g_ref, side, zone), weight, 1, 1)
            total = term if total is None else total + term
        for step in range(NL):
            ref[step] = total[:, step * DH : (step + 1) * DH].astype(BF16)


def weight_kernel(g_ref, own_ref, other_ref, out_ref):
    core = lax.axis_index("core")
    own = own_ref[...].reshape(NL * DH, TOK)
    other = other_ref[...].reshape(NL * DH, TOK)
    for step in range(NZ):
        total = dot(own, block(g_ref, core, step), 1, 0)
        total = total + dot(other, block(g_ref, 1 - core, step), 1, 0)
        out_ref[:, step] = total.reshape(NL, DH, BLK).astype(BF16)


def call(kernel, outs, flops, moved, operands):
    return pl.pallas_call(
        kernel,
        out_shape=outs,
        in_specs=[pl.BlockSpec(memory_space=pltpu.VMEM)] * len(operands),
        out_specs=jax.tree.map(lambda _: pl.BlockSpec(memory_space=pltpu.VMEM), outs),
        compiler_params=pltpu.CompilerParams(vmem_limit_bytes=VMEM_LIMIT),
        cost_estimate=pl.CostEstimate(flops=flops, bytes_accessed=moved, transcendentals=0),
    )(*operands)


def cross(entry):
    pairs = [(at * NL + low, low * NL + at) for at in range(NX) for low in range(NL)]
    return lax.ppermute(entry, ("x", "zl"), pairs)


def flip(entry, step):
    return lax.ppermute(entry, "zl", [(at, at ^ step) for at in range(NL)])


def share(entry, axis, size):
    copies = jnp.broadcast_to(entry[None], (size,) + entry.shape)
    return lax.all_to_all(copies, axis, 0, 0, tiled=True)


def swap_cores(entry):
    return lax.ppermute(entry, "core", [(0, 1), (1, 0)])


def shards(query_input, key_input, value_input, query_gain, key_gain, out_weight, grad_output):
    query_gain = query_gain.reshape(1, DH)
    key_gain = key_gain.reshape(1, DH)
    shape = jax.ShapeDtypeStruct

    rows = grad_output.shape[0]
    groups = NC * NL
    pieces = call(cut_kernel, shape((groups, rows, WIDE), BF16), 0, 1 << 18, (grad_output,))
    exchanged = lax.all_to_all(pieces, ("core", "zl"), 0, 0, tiled=True)
    gathered = lax.all_gather(exchanged, "y", axis=0)

    mixed, attention = call(
        forward_kernel,
        (shape((DH, TOK), BF16), shape((IMAGES, PATCH, PATCH), F32)),
        2 * 2 * IMAGES * PATCH * PATCH * DH,
        1 << 20,
        (query_input, key_input, value_input, query_gain, key_gain),
    )
    exchanged, out_weight = lax.optimization_barrier((exchanged, out_weight))
    zones = share(cross(out_weight), "zh", NZ)
    mixed, zones = lax.optimization_barrier((mixed, zones))
    mixed_own = share(mixed, "zl", NL)
    own = lax.all_gather(zones, "x", axis=0)
    mixed_own, own = lax.optimization_barrier((mixed_own, own))
    mixed_other = swap_cores(mixed_own)
    gathered, own, mixed_other = lax.optimization_barrier((gathered, own, mixed_other))

    half = (NL, TOK, DH)
    keep, send = call(
        heads_kernel,
        (shape(half, BF16), shape(half, BF16)),
        2 * TOK * NY * DH * WIDE,
        4 << 20,
        (gathered, own),
    )
    gathered, send = lax.optimization_barrier((gathered, send))
    received = swap_cores(send)
    partial = call(
        weight_kernel,
        shape((NL, NZ, DH, BLK), BF16),
        2 * TOK * NY * DH * WIDE,
        5 << 20,
        (gathered, mixed_own, mixed_other),
    )
    spread = lax.all_to_all(partial, "x", 0, 0, tiled=True)
    summed = [
        (keep[step].astype(F32) + received[step].astype(F32)).astype(BF16) for step in range(NL)
    ]
    grad_heads = [summed[0]] + [flip(summed[step], step) for step in range(1, NL)]
    by_zone = sum(spread[part].astype(F32) for part in range(NX)).astype(BF16)
    last = lax.all_to_all(by_zone, "zh", 0, 0, tiled=True)
    grad_weight = cross(sum(last[zone].astype(F32) for zone in range(NZ)).astype(BF16))

    grad_query, grad_key, grad_value = call(
        backward_kernel,
        (shape((TOK, DH), BF16),) * 3,
        5 * 2 * IMAGES * PATCH * PATCH * DH,
        2 << 20,
        (query_input, key_input, value_input, query_gain, key_gain, attention, *grad_heads),
    )
    return grad_query, grad_key, grad_value, grad_weight


def solution(mesh):
    axes = ("zh", "x", "core", "y", "zl")
    fine = Mesh(mesh.devices.reshape(NZ, NX, NC, NY, NL), axes)
    tokens, heads = ("zh", "x", "core"), ("y", "zl")
    in_specs = (
        P(tokens, heads),
        P(tokens, heads),
        P(tokens, heads),
        P(),
        P(),
        P(heads, tokens),
        P(tokens + heads, None),
    )
    out_specs = (P(tokens, heads), P(tokens, heads), P(tokens, heads), P(heads, tokens))
    return jax.shard_map(shards, mesh=fine, in_specs=in_specs, out_specs=out_specs, check_vma=False)
```

```python
import functools
import math

import jax
import jax.numpy as jnp
from jax import lax
from jax.experimental import pallas as pl
from jax.experimental.pallas import tpu as pltpu
from jax.sharding import Mesh
from jax.sharding import PartitionSpec as P

DH = 128
PATCH = 256
IMAGES = 2
TOK = 512
NZ, NX, NC, NY, NL = 3, 4, 2, 8, 4
BLK = 256
WIDE = NZ * BLK
epsilon = 1e-06
F32 = jnp.float32
BF16 = jnp.bfloat16
VMEM_LIMIT = 12 * 1024 * 1024
SCALING = 1.0 / math.sqrt(DH)


def dot(a, b, ca, cb):
    return lax.dot_general(a, b, (((ca,), (cb,)), ((), ())), preferred_element_type=F32)


def normalize(inputs):
    inputs = inputs.astype(F32)
    average = jnp.mean(inputs, axis=-1, keepdims=True)
    centred = inputs - average
    inverse = lax.rsqrt(jnp.mean(centred * centred, axis=-1, keepdims=True) + epsilon)
    return centred * inverse, inverse


def norm_back(gradient, unit_rows, inverse, gain):
    scaled = gradient * gain
    return (
        scaled
        - jnp.mean(scaled, axis=-1, keepdims=True)
        - unit_rows * jnp.mean(scaled * unit_rows, axis=-1, keepdims=True)
    ) * inverse


def cut_kernel(go_ref, cut_ref):
    for zone in range(NZ):
        for low in range(NL):
            for core in range(NC):
                source = ((zone * NL + low) * NC + core) * BLK
                piece = go_ref[:, source : source + BLK]
                cut_ref[core * NL + low, :, zone * BLK : (zone + 1) * BLK] = piece


def forward_kernel(q_ref, k_ref, v_ref, qg_ref, kg_ref, mixed_ref, att_ref):
    for image in range(IMAGES):
        rows = pl.ds(image * PATCH, PATCH)
        query_low = (normalize(q_ref[rows, :])[0] * qg_ref[...]).astype(BF16)
        key_low = (normalize(k_ref[rows, :])[0] * kg_ref[...]).astype(BF16)
        exponent = jnp.exp(dot(query_low, key_low, 1, 1) * SCALING)
        attention = exponent / jnp.sum(exponent, axis=-1, keepdims=True)
        att_ref[image] = attention
        mixed = dot(v_ref[rows, :], attention.astype(BF16), 0, 1)
        mixed_ref[:, rows] = mixed.astype(BF16)


def backward_kernel(q_ref, k_ref, v_ref, qg_ref, kg_ref, att_ref, *refs):
    gh_refs, (dq_ref, dk_ref, dv_ref) = refs[:NL], refs[NL:]
    for image in range(IMAGES):
        rows = pl.ds(image * PATCH, PATCH)
        total = gh_refs[0][rows, :].astype(F32)
        for part in range(1, NL):
            total = total + gh_refs[part][rows, :].astype(F32)
        grad_heads = total.astype(BF16)
        query_unit, query_inv = normalize(q_ref[rows, :])
        key_unit, key_inv = normalize(k_ref[rows, :])
        query_low = (query_unit * qg_ref[...]).astype(BF16)
        key_low = (key_unit * kg_ref[...]).astype(BF16)
        attention = att_ref[image]
        dv_ref[rows, :] = dot(attention.astype(BF16), grad_heads, 0, 0).astype(BF16)
        grad_attention = dot(grad_heads, v_ref[rows, :], 1, 1)
        row_delta = jnp.sum(attention * grad_attention, axis=-1, keepdims=True)
        grad_scores = (attention * (grad_attention - row_delta)).astype(BF16)
        grad_qn = dot(grad_scores, key_low, 1, 0) * SCALING
        grad_kn = dot(grad_scores, query_low, 0, 0) * SCALING
        dq_ref[rows, :] = norm_back(grad_qn, query_unit, query_inv, qg_ref[...]).astype(BF16)
        dk_ref[rows, :] = norm_back(grad_kn, key_unit, key_inv, kg_ref[...]).astype(BF16)


def block(ref, side, zone):
    columns = slice(zone * BLK, (zone + 1) * BLK)
    return ref[:, pl.ds(side * NL, NL), :, columns].reshape(TOK, BLK)


def heads_kernel(g_ref, own_ref, keep_ref, send_ref):
    core, low = lax.axis_index("core"), lax.axis_index("zl")
    for ref, side in ((send_ref, 1 - core), (keep_ref, core)):
        total = None
        for zone in range(NZ):
            weight = jnp.concatenate([own_ref[low ^ step, zone] for step in range(NL)], axis=0)
            term = dot(block(g_ref, side, zone), weight, 1, 1)
            total = term if total is None else total + term
        for step in range(NL):
            ref[step] = total[:, step * DH : (step + 1) * DH].astype(BF16)


def weight_kernel(g_ref, own_ref, other_ref, out_ref):
    core = lax.axis_index("core")
    own = own_ref[...].reshape(NL * DH, TOK)
    other = other_ref[...].reshape(NL * DH, TOK)
    for step in range(NZ):
        total = dot(own, block(g_ref, core, step), 1, 0)
        total = total + dot(other, block(g_ref, 1 - core, step), 1, 0)
        out_ref[:, step] = total.reshape(NL, DH, BLK).astype(BF16)


def call(kernel, outs, flops, moved, operands):
    return pl.pallas_call(
        kernel,
        out_shape=outs,
        in_specs=[pl.BlockSpec(memory_space=pltpu.VMEM)] * len(operands),
        out_specs=jax.tree.map(lambda _: pl.BlockSpec(memory_space=pltpu.VMEM), outs),
        compiler_params=pltpu.CompilerParams(vmem_limit_bytes=VMEM_LIMIT),
        cost_estimate=pl.CostEstimate(flops=flops, bytes_accessed=moved, transcendentals=0),
    )(*operands)


def cross(entry):
    pairs = [(at * NL + low, low * NL + at) for at in range(NX) for low in range(NL)]
    return lax.ppermute(entry, ("x", "zl"), pairs)


def flip(entry, step):
    return lax.ppermute(entry, "zl", [(at, at ^ step) for at in range(NL)])


def share(entry, axis, size):
    copies = jnp.broadcast_to(entry[None], (size,) + entry.shape)
    return lax.all_to_all(copies, axis, 0, 0, tiled=True)


def swap_cores(entry):
    return lax.ppermute(entry, "core", [(0, 1), (1, 0)])


def shards(query_input, key_input, value_input, query_gain, key_gain, out_weight, grad_output):
    query_gain = query_gain.reshape(1, DH)
    key_gain = key_gain.reshape(1, DH)
    shape = jax.ShapeDtypeStruct

    rows = grad_output.shape[0]
    groups = NC * NL
    pieces = call(cut_kernel, shape((groups, rows, WIDE), BF16), 0, 1 << 18, (grad_output,))
    exchanged = lax.all_to_all(pieces, ("core", "zl"), 0, 0, tiled=True)
    gathered = lax.all_gather(exchanged, "y", axis=0)

    mixed, attention = call(
        forward_kernel,
        (shape((DH, TOK), BF16), shape((IMAGES, PATCH, PATCH), F32)),
        2 * 2 * IMAGES * PATCH * PATCH * DH,
        1 << 20,
        (query_input, key_input, value_input, query_gain, key_gain),
    )
    exchanged, out_weight = lax.optimization_barrier((exchanged, out_weight))
    zones = share(cross(out_weight), "zh", NZ)
    mixed, zones = lax.optimization_barrier((mixed, zones))
    mixed_own = share(mixed, "zl", NL)
    own = lax.all_gather(zones, "x", axis=0)
    mixed_own, own = lax.optimization_barrier((mixed_own, own))
    mixed_other = swap_cores(mixed_own)
    gathered, own, mixed_other = lax.optimization_barrier((gathered, own, mixed_other))

    half = (NL, TOK, DH)
    keep, send = call(
        heads_kernel,
        (shape(half, BF16), shape(half, BF16)),
        2 * TOK * NY * DH * WIDE,
        4 << 20,
        (gathered, own),
    )
    gathered, send = lax.optimization_barrier((gathered, send))
    received = swap_cores(send)
    partial = call(
        weight_kernel,
        shape((NL, NZ, DH, BLK), BF16),
        2 * TOK * NY * DH * WIDE,
        5 << 20,
        (gathered, mixed_own, mixed_other),
    )
    spread = lax.all_to_all(partial, "x", 0, 0, tiled=True)
    summed = [
        (keep[step].astype(F32) + received[step].astype(F32)).astype(BF16) for step in range(NL)
    ]
    grad_heads = [summed[0]] + [flip(summed[step], step) for step in range(1, NL)]
    spread, *grad_heads = lax.optimization_barrier((spread, *grad_heads))
    by_zone = sum(spread[part].astype(F32) for part in range(NX)).astype(BF16)
    last = lax.all_to_all(by_zone, "zh", 0, 0, tiled=True)
    grad_weight = cross(sum(last[zone].astype(F32) for zone in range(NZ)).astype(BF16))

    grad_query, grad_key, grad_value = call(
        backward_kernel,
        (shape((TOK, DH), BF16),) * 3,
        5 * 2 * IMAGES * PATCH * PATCH * DH,
        2 << 20,
        (query_input, key_input, value_input, query_gain, key_gain, attention, *grad_heads),
    )
    return grad_query, grad_key, grad_value, grad_weight


def solution(mesh):
    axes = ("zh", "x", "core", "y", "zl")
    fine = Mesh(mesh.devices.reshape(NZ, NX, NC, NY, NL), axes)
    tokens, heads = ("zh", "x", "core"), ("y", "zl")
    in_specs = (
        P(tokens, heads),
        P(tokens, heads),
        P(tokens, heads),
        P(),
        P(),
        P(heads, tokens),
        P(tokens + heads, None),
    )
    out_specs = (P(tokens, heads), P(tokens, heads), P(tokens, heads), P(heads, tokens))
    return jax.shard_map(shards, mesh=fine, in_specs=in_specs, out_specs=out_specs, check_vma=False)
```

```python
import functools
import math

import jax
import jax.numpy as jnp
from jax import lax
from jax.experimental import pallas as pl
from jax.experimental.pallas import tpu as pltpu
from jax.sharding import Mesh
from jax.sharding import PartitionSpec as P

DH = 128
PATCH = 256
IMAGES = 2
TOK = 512
NZ, NX, NC, NY, NL = 3, 4, 2, 8, 4
BLK = 256
WIDE = NZ * BLK
epsilon = 1e-06
F32 = jnp.float32
BF16 = jnp.bfloat16
VMEM_LIMIT = 12 * 1024 * 1024
SCALING = 1.0 / math.sqrt(DH)


def dot(a, b, ca, cb):
    return lax.dot_general(a, b, (((ca,), (cb,)), ((), ())), preferred_element_type=F32)


def normalize(inputs):
    inputs = inputs.astype(F32)
    average = jnp.mean(inputs, axis=-1, keepdims=True)
    centred = inputs - average
    inverse = lax.rsqrt(jnp.mean(centred * centred, axis=-1, keepdims=True) + epsilon)
    return centred * inverse, inverse


def norm_back(gradient, unit_rows, inverse, gain):
    scaled = gradient * gain
    return (
        scaled
        - jnp.mean(scaled, axis=-1, keepdims=True)
        - unit_rows * jnp.mean(scaled * unit_rows, axis=-1, keepdims=True)
    ) * inverse


def cut_kernel(go_ref, cut_ref):
    for zone in range(NZ):
        for low in range(NL):
            for core in range(NC):
                source = ((zone * NL + low) * NC + core) * BLK
                piece = go_ref[:, source : source + BLK]
                cut_ref[core * NL + low, :, zone * BLK : (zone + 1) * BLK] = piece


def forward_kernel(q_ref, k_ref, v_ref, qg_ref, kg_ref, mixed_ref, att_ref):
    for image in range(IMAGES):
        rows = pl.ds(image * PATCH, PATCH)
        query_low = (normalize(q_ref[rows, :])[0] * qg_ref[...]).astype(BF16)
        key_low = (normalize(k_ref[rows, :])[0] * kg_ref[...]).astype(BF16)
        exponent = jnp.exp(dot(query_low, key_low, 1, 1) * SCALING)
        attention = exponent / jnp.sum(exponent, axis=-1, keepdims=True)
        att_ref[image] = attention
        mixed = dot(v_ref[rows, :], attention.astype(BF16), 0, 1)
        mixed_ref[:, rows] = mixed.astype(BF16)


def backward_kernel(
    q_ref, k_ref, v_ref, qg_ref, kg_ref, att_ref, gh_ref, dq_ref, dk_ref, dv_ref
):
    for image in range(IMAGES):
        rows = pl.ds(image * PATCH, PATCH)
        grad_heads = gh_ref[rows, :]
        query_unit, query_inv = normalize(q_ref[rows, :])
        key_unit, key_inv = normalize(k_ref[rows, :])
        query_low = (query_unit * qg_ref[...]).astype(BF16)
        key_low = (key_unit * kg_ref[...]).astype(BF16)
        attention = att_ref[image]
        dv_ref[rows, :] = dot(attention.astype(BF16), grad_heads, 0, 0).astype(BF16)
        grad_attention = dot(grad_heads, v_ref[rows, :], 1, 1)
        row_delta = jnp.sum(attention * grad_attention, axis=-1, keepdims=True)
        grad_scores = (attention * (grad_attention - row_delta)).astype(BF16)
        grad_qn = dot(grad_scores, key_low, 1, 0) * SCALING
        grad_kn = dot(grad_scores, query_low, 0, 0) * SCALING
        dq_ref[rows, :] = norm_back(grad_qn, query_unit, query_inv, qg_ref[...]).astype(BF16)
        dk_ref[rows, :] = norm_back(grad_kn, key_unit, key_inv, kg_ref[...]).astype(BF16)


def block(ref, side, zone):
    columns = slice(zone * BLK, (zone + 1) * BLK)
    return ref[:, pl.ds(side * NL, NL), :, columns].reshape(TOK, BLK)


def heads_kernel(g_ref, own_ref, keep_ref, send_ref):
    core = lax.axis_index("core")
    for ref, side in ((send_ref, 1 - core), (keep_ref, core)):
        total = None
        for step in range(NZ):
            rows = block(g_ref, side, step)
            term = dot(rows, own_ref[:, step].reshape(NL * DH, BLK), 1, 1)
            total = term if total is None else total + term
        for head in range(NL):
            ref[head] = total[:, head * DH : (head + 1) * DH].astype(BF16)


def weight_kernel(g_ref, own_ref, other_ref, out_ref):
    core = lax.axis_index("core")
    own = own_ref[...].reshape(NL * DH, TOK)
    other = other_ref[...].reshape(NL * DH, TOK)
    for step in range(NZ):
        total = dot(own, block(g_ref, core, step), 1, 0)
        total = total + dot(other, block(g_ref, 1 - core, step), 1, 0)
        out_ref[:, step] = total.reshape(NL, DH, BLK).astype(BF16)


def call(kernel, outs, flops, moved, operands):
    return pl.pallas_call(
        kernel,
        out_shape=outs,
        in_specs=[pl.BlockSpec(memory_space=pltpu.VMEM)] * len(operands),
        out_specs=jax.tree.map(lambda _: pl.BlockSpec(memory_space=pltpu.VMEM), outs),
        compiler_params=pltpu.CompilerParams(vmem_limit_bytes=VMEM_LIMIT),
        cost_estimate=pl.CostEstimate(flops=flops, bytes_accessed=moved, transcendentals=0),
    )(*operands)


def cross(entry):
    pairs = [(at * NL + low, low * NL + at) for at in range(NX) for low in range(NL)]
    return lax.ppermute(entry, ("x", "zl"), pairs)


def share(entry, axis, size):
    copies = jnp.broadcast_to(entry[None], (size,) + entry.shape)
    return lax.all_to_all(copies, axis, 0, 0, tiled=True)


def swap_cores(entry):
    return lax.ppermute(entry, "core", [(0, 1), (1, 0)])


def shards(query_input, key_input, value_input, query_gain, key_gain, out_weight, grad_output):
    query_gain = query_gain.reshape(1, DH)
    key_gain = key_gain.reshape(1, DH)
    shape = jax.ShapeDtypeStruct

    rows = grad_output.shape[0]
    groups = NC * NL
    pieces = call(cut_kernel, shape((groups, rows, WIDE), BF16), 0, 1 << 18, (grad_output,))
    exchanged = lax.all_to_all(pieces, ("core", "zl"), 0, 0, tiled=True)
    gathered = lax.all_gather(exchanged, "y", axis=0)

    mixed, attention = call(
        forward_kernel,
        (shape((DH, TOK), BF16), shape((IMAGES, PATCH, PATCH), F32)),
        2 * 2 * IMAGES * PATCH * PATCH * DH,
        1 << 20,
        (query_input, key_input, value_input, query_gain, key_gain),
    )
    exchanged, out_weight = lax.optimization_barrier((exchanged, out_weight))
    zones = share(cross(out_weight), "zh", NZ)
    mixed, zones = lax.optimization_barrier((mixed, zones))
    mixed_own = share(mixed, "zl", NL)
    own = lax.all_gather(zones, "x", axis=0)
    mixed_own, own = lax.optimization_barrier((mixed_own, own))
    mixed_other = swap_cores(mixed_own)
    gathered, own = lax.optimization_barrier((gathered, own))

    half = (NL, TOK, DH)
    keep, send = call(
        heads_kernel,
        (shape(half, BF16), shape(half, BF16)),
        2 * TOK * NY * DH * WIDE,
        4 << 20,
        (gathered, own),
    )
    gathered, send = lax.optimization_barrier((gathered, send))
    received = swap_cores(send)
    partial = call(
        weight_kernel,
        shape((NL, NZ, DH, BLK), BF16),
        2 * TOK * NY * DH * WIDE,
        5 << 20,
        (gathered, mixed_own, mixed_other),
    )
    spread = lax.all_to_all(partial, "x", 0, 0, tiled=True)
    summed = (keep.astype(F32) + received.astype(F32)).astype(BF16)
    grad_heads = lax.psum_scatter(summed, "zl", scatter_dimension=0, tiled=True)
    by_zone = sum(spread[part].astype(F32) for part in range(NX)).astype(BF16)
    last = lax.all_to_all(by_zone, "zh", 0, 0, tiled=True)
    grad_weight = cross(sum(last[zone].astype(F32) for zone in range(NZ)).astype(BF16))

    grad_query, grad_key, grad_value = call(
        backward_kernel,
        (shape((TOK, DH), BF16),) * 3,
        5 * 2 * IMAGES * PATCH * PATCH * DH,
        2 << 20,
        (query_input, key_input, value_input, query_gain, key_gain, attention, grad_heads.reshape(TOK, DH)),
    )
    return grad_query, grad_key, grad_value, grad_weight


def solution(mesh):
    axes = ("zh", "x", "core", "y", "zl")
    fine = Mesh(mesh.devices.reshape(NZ, NX, NC, NY, NL), axes)
    tokens, heads = ("zh", "x", "core"), ("y", "zl")
    in_specs = (
        P(tokens, heads),
        P(tokens, heads),
        P(tokens, heads),
        P(),
        P(),
        P(heads, tokens),
        P(tokens + heads, None),
    )
    out_specs = (P(tokens, heads), P(tokens, heads), P(tokens, heads), P(heads, tokens))
    return jax.shard_map(shards, mesh=fine, in_specs=in_specs, out_specs=out_specs, check_vma=False)
```
